128 devices in a mesh: gx: 8 (over x, core), gy: 16 (over z, y).
Axes of the slice: x: 4, y: 4, z: 4, core: 2. Of those that a mesh axis runs over, the one named last changes fastest.
Arguments:
- vectors: float32 [4, 262144], P(None, ('gx', 'gy')), may hold values from -6 to 6
- cluster_order: int32 [128, 2048], P(('gx', 'gy')), may hold values from 0 to 2047, each once within a row
- near_blocks: float32 [32, 64, 128, 9, 128], P('gx', 'gy'), may hold values from -0.1875 to 0.1875
- leaf_basis: float32 [32, 64, 128, 64], P('gx', 'gy'), may hold values from -0.5 to 0.5
- couple_leaf: float32 [32, 64, 64, 27, 64], P('gx', 'gy'), may hold values from -0.15625 to 0.15625
- transfer_leaf: float32 [32, 64, 64, 64], P('gx', 'gy'), may hold values from -0.5 to 0.5
- couple_node: float32 [16, 32, 64, 27, 64], P('gx', 'gy'), may hold values from -0.15625 to 0.15625
- transfer_node: float32 [16, 32, 64, 64], P('gx', 'gy'), may hold values from -0.5 to 0.5
- transfer_device: float32 [8, 16, 64, 64], P('gx', 'gy'), may hold values from -0.5 to 0.5
- couple_upper: float32 [128, 35, 64, 64], P(('gx', 'gy')), may hold values from -0.15625 to 0.15625
- pair_list: int32 [2, 128, 35], P(None, ('gx', 'gy')), may hold values from 0 to 160, as said below
Outputs:
- product: float32 [4, 262144], P(None, ('gx', 'gy'))
The draws below stay inside these ranges and needn't reach their ends.
Inputs may be any that keep to these rules, and one draw needn't show every extreme that they name: pair_list[0, d, k] is the target box and pair_list[1, d, k] the source box of coupling slot (d, k), numbered as in the reference program. Every admissible pair appears in exactly one slot: device boxes whose parents are equal or adjacent (also diagonally) but which are not themselves adjacent, and level 3 boxes that are not adjacent. A slot with target 160 is empty and has source 0.
All inputs are finite; a program needn't handle non-finite values.
Results may differ from the reference program's by a relative error of at most 0.000054.
Values sent between devices are 32-bit elements; how exact they have to be, the bound alone decides.
A program may use at most 128 MiB of HBM per device.

```python
import jax
import jax.numpy as jnp
from jax import lax

LEAF = 128
RANK = 64
NVEC = 4
BLK = 4
PTS_DEV = 2048
POINTS = 262144
LX = 32
LY = 64
NODES = 160
SLOTS = 35
N_GX = 8
N_GY = 16
DEVICES = 128


def draw_pair_list(key, part):
    key = jax.random.fold_in(key, 17)
    first_extent, second_extent = (N_GX, N_GY)
    devices = first_extent * second_extent
    row_index = jnp.arange(first_extent, dtype=jnp.int32)[:, None, None, None]
    column_index = jnp.arange(second_extent, dtype=jnp.int32)[None, :, None, None]
    step_row = jnp.arange(6, dtype=jnp.int32)[None, None, :, None]
    step_column = jnp.arange(6, dtype=jnp.int32)[None, None, None, :]
    source_row = 2 * (row_index // 2) - 2 + step_row
    source_column = 2 * (column_index // 2) - 2 + step_column
    inside = (source_row >= 0) & (source_row < first_extent) & (source_column >= 0) & (source_column < second_extent)
    distant = (jnp.abs(source_row - row_index) > 1) | (jnp.abs(source_column - column_index) > 1)
    shape_low = (first_extent, second_extent, 6, 6)
    valid_low = jnp.broadcast_to(inside & distant, shape_low).reshape(-1).astype(jnp.int32)
    target_low = jnp.broadcast_to(row_index * second_extent + column_index, shape_low).reshape(-1)
    source_low = jnp.broadcast_to(jnp.clip(source_row, 0, first_extent - 1) * second_extent + jnp.clip(source_column, 0, second_extent - 1), shape_low).reshape(-1)
    half_first, half_second = (first_extent // 2, second_extent // 2)
    group_row = jnp.arange(half_first, dtype=jnp.int32)[:, None, None, None]
    group_column = jnp.arange(half_second, dtype=jnp.int32)[None, :, None, None]
    other_row = jnp.arange(half_first, dtype=jnp.int32)[None, None, :, None]
    other_column = jnp.arange(half_second, dtype=jnp.int32)[None, None, None, :]
    shape_up = (half_first, half_second, half_first, half_second)
    valid_up = jnp.broadcast_to((jnp.abs(group_row - other_row) > 1) | (jnp.abs(group_column - other_column) > 1), shape_up).reshape(-1).astype(jnp.int32)
    target_up = jnp.broadcast_to(devices + group_row * half_second + group_column, shape_up).reshape(-1)
    source_up = jnp.broadcast_to(devices + other_row * half_second + other_column, shape_up).reshape(-1)
    valid = jnp.concatenate([valid_low, valid_up], 0)
    targets = jnp.concatenate([target_low, target_up], 0)
    sources = jnp.concatenate([source_low, source_up], 0)
    total = valid.shape[0]
    ranking = jax.random.permutation(key, total).astype(jnp.int32)
    score = (1 - valid) * total + ranking
    chosen = jnp.argsort(score)[:devices * SLOTS]
    keeping = valid[chosen]
    target_sel = jnp.where(keeping == 1, targets[chosen], NODES)
    source_sel = jnp.where(keeping == 1, sources[chosen], 0)
    return jnp.stack([target_sel, source_sel], 0).reshape(2, devices, SLOTS).astype(jnp.int32)


def block_levels(own_key, shape, cuts, least, largest):
    loudness = 1.0
    for dim, blocks in cuts:
        steps = jax.random.uniform(jax.random.fold_in(jax.random.fold_in(own_key, 6), dim), (blocks,), jnp.float32, least / len(cuts), largest / len(cuts))
        loudness = loudness * jnp.repeat(jnp.exp(steps), shape[dim] // blocks).reshape((-1,) + (1,) * (len(shape) - 1 - dim))
    return loudness


def gaussian(rng, dims, deviation, limit, cuts=(), kind=jnp.bfloat16):
    factor_of = block_levels(rng, dims, cuts, -0.22, 0.18) if cuts else 1.0
    values = jax.random.normal(rng, dims, jnp.float32) * deviation * factor_of
    return jnp.minimum(jnp.maximum(values, -limit), limit).astype(kind)


def setup_inputs(seed: int = 0) -> dict:
    seeds = jax.random.split(jax.random.key(seed), 12)
    return {
        "vectors": gaussian(seeds[0], (NVEC, POINTS), 1.0, 6.0, ((1, 128),), jnp.float32),
        "cluster_order": jax.vmap(lambda own: jax.random.permutation(own, PTS_DEV))(jax.random.split(seeds[1], DEVICES)).reshape((DEVICES, PTS_DEV)).astype(jnp.int32),
        "near_blocks": gaussian(seeds[2], (LX, LY, LEAF, 9, LEAF), (9 * LEAF) ** -0.5, 0.1875, ((0, 8), (1, 16)), jnp.float32),
        "leaf_basis": gaussian(seeds[3], (LX, LY, LEAF, RANK), LEAF ** -0.5, 0.5, ((0, 8), (1, 16)), jnp.float32),
        "couple_leaf": gaussian(seeds[4], (LX, LY, RANK, 27, RANK), (27 * RANK) ** -0.5, 0.15625, ((0, 8), (1, 16)), jnp.float32),
        "transfer_leaf": gaussian(seeds[5], (LX, LY, RANK, RANK), (2 * RANK) ** -0.5, 0.5, ((0, 8), (1, 16)), jnp.float32),
        "couple_node": gaussian(seeds[6], (LX // 2, LY // 2, RANK, 27, RANK), (27 * RANK) ** -0.5, 0.15625, ((0, 8), (1, 16)), jnp.float32),
        "transfer_node": gaussian(seeds[7], (LX // 2, LY // 2, RANK, RANK), (2 * RANK) ** -0.5, 0.5, ((0, 8), (1, 16)), jnp.float32),
        "transfer_device": gaussian(seeds[8], (N_GX, N_GY, RANK, RANK), (2 * RANK) ** -0.5, 0.5, ((0, 8), (1, 16)), jnp.float32),
        "couple_upper": gaussian(seeds[9], (DEVICES, SLOTS, RANK, RANK), (27 * RANK) ** -0.5, 0.15625, ((0, 128),), jnp.float32),
        "pair_list": draw_pair_list(jax.random.fold_in(seeds[11], 71), 0),
    }


precise = lax.Precision.HIGHEST


def slots_table():
    result_table = []
    for row_parity in range(2):
        row_list = []
        for column_parity in range(2):
            cell_list = []
            for first in range(6):
                for second in range(6):
                    nearby = row_parity + 1 <= first <= row_parity + 3 and column_parity + 1 <= second <= column_parity + 3
                    if not nearby:
                        cell_list.append((first, second))
            row_list.append(cell_list)
        result_table.append(row_list)
    return result_table


def far_block(padded, couple, vec_count, rank_width):
    row_count, column_count = couple.shape[0], couple.shape[1]
    slot_count = couple.shape[3]
    half_rows, half_columns = row_count // 2, column_count // 2
    windows = {}
    for first in range(6):
        for second in range(6):
            windows[(first, second)] = padded[first:first + 2 * half_rows - 1:2, second:second + 2 * half_columns - 1:2].reshape(half_rows, half_columns, vec_count, rank_width)
    layout = slots_table()
    parity_rows = []
    for row_parity in range(2):
        parity_cols = [jnp.stack([windows[position] for position in layout[row_parity][column_parity]], 3) for column_parity in range(2)]
        parity_rows.append(jnp.stack(parity_cols, 2))
    stacked = jnp.stack(parity_rows, 1).reshape(row_count, column_count, vec_count, slot_count * rank_width)
    blocks = couple.reshape(row_count, column_count, rank_width, slot_count * rank_width)
    return jnp.einsum("abrk,abnk->abnr", blocks, stacked, precision=precise)


def lift(child, transfer):
    row_count, column_count = child.shape[0], child.shape[1]
    shaped = child.reshape(row_count // 2, 2, column_count // 2, 2, child.shape[2], child.shape[3])
    matrix = transfer.reshape(row_count // 2, 2, column_count // 2, 2, transfer.shape[2], transfer.shape[3])
    return jnp.einsum("uavbrq,uavbnr->uvnq", matrix, shaped, precision=precise)


def push(parent, transfer):
    matrix = transfer.reshape(parent.shape[0], 2, parent.shape[1], 2, transfer.shape[2], transfer.shape[3])
    result = jnp.einsum("uavbrq,uvnq->uavbnr", matrix, parent, precision=precise)
    return result.reshape(2 * parent.shape[0], 2 * parent.shape[1], parent.shape[2], parent.shape[3])


def near_part(padded, near_blocks, vec_count, leaf_size):
    row_count, column_count = near_blocks.shape[0], near_blocks.shape[1]
    pieces = [padded[1 + row_shift:1 + row_shift + row_count, 1 + column_shift:1 + column_shift + column_count].reshape(row_count, column_count, vec_count, leaf_size) for row_shift in (-1, 0, 1) for column_shift in (-1, 0, 1)]
    stacked = jnp.stack(pieces, 3).reshape(row_count, column_count, vec_count, 9 * leaf_size)
    blocks = near_blocks.reshape(row_count, column_count, leaf_size, 9 * leaf_size)
    return jnp.einsum("abik,abnk->abni", blocks, stacked, precision=precise)


def pad_grid(values, depth):
    flattened = values.reshape(values.shape[0], values.shape[1], -1)
    return jnp.pad(flattened, ((depth, depth), (depth, depth), (0, 0)))


def reference(vectors, cluster_order, near_blocks, leaf_basis, couple_leaf, transfer_leaf, couple_node, transfer_node, transfer_device, couple_upper, pair_list):
    per_device = cluster_order.shape[1]
    feature_width = NVEC * RANK
    grouped = vectors.reshape(NVEC, DEVICES, per_device)
    clustered = jax.vmap(lambda block_values, indices: block_values[:, indices], in_axes=(1, 0), out_axes=1)(grouped, cluster_order)
    leaves = clustered.reshape(NVEC, N_GX, N_GY, BLK, BLK, LEAF).transpose(1, 3, 2, 4, 0, 5).reshape(N_GX * BLK, N_GY * BLK, NVEC, LEAF)
    up_leaf = jnp.einsum("abpq,abnp->abnq", leaf_basis, leaves, precision=precise)
    up_node = lift(up_leaf, transfer_leaf)
    up_device = lift(up_node, transfer_node)
    up_group = lift(up_device, transfer_device)
    coefficient_table = jnp.concatenate([up_device.reshape(DEVICES, feature_width), up_group.reshape(-1, feature_width)], 0)
    picked = coefficient_table[pair_list[1]].reshape(DEVICES, SLOTS, NVEC, RANK)
    products = jnp.einsum("dsrq,dsnq->dsnr", couple_upper, picked, precision=precise)
    upper_sums = jax.ops.segment_sum(products.reshape(-1, NVEC, RANK), pair_list[0].reshape(-1), num_segments=NODES + 1)[:NODES]
    down_device = upper_sums[:DEVICES].reshape(N_GX, N_GY, NVEC, RANK) + push(upper_sums[DEVICES:].reshape(N_GX // 2, N_GY // 2, NVEC, RANK), transfer_device)
    down_node = far_block(pad_grid(up_node, 2), couple_node, NVEC, RANK) + push(down_device, transfer_node)
    down_leaf = far_block(pad_grid(up_leaf, 2), couple_leaf, NVEC, RANK) + push(down_node, transfer_leaf)
    y_leaf = jnp.einsum("abpq,abnq->abnp", leaf_basis, down_leaf, precision=precise) + near_part(pad_grid(leaves, 1), near_blocks, NVEC, LEAF)
    ordered = y_leaf.reshape(N_GX, BLK, N_GY, BLK, NVEC, LEAF).transpose(4, 0, 2, 1, 3, 5).reshape(NVEC, DEVICES, per_device)
    restored = jax.vmap(lambda block_values, indices: jnp.zeros_like(block_values).at[:, indices].set(block_values), in_axes=(1, 0), out_axes=1)(ordered, cluster_order)
    return restored.reshape(NVEC, DEVICES * per_device)
```

```python
import functools

import jax
import jax.numpy as jnp
from jax import lax
from jax.experimental import pallas as pl
from jax.experimental.pallas import tpu as pltpu
from jax.sharding import PartitionSpec as P

F32 = jnp.float32
BF16 = jnp.bfloat16
MESH = pl.DeviceIdType.MESH
NT = (((1,), (1,)), ((), ()))
NN = (((1,), (0,)), ((), ()))
DIRECTIONS = [(dx, dy) for dx in (-1, 0, 1) for dy in (-1, 0, 1) if (dx, dy) != (0, 0)]


def slots_of(s, w):
    return [
        (i, j)
        for i in range(6)
        for j in range(6)
        if not (s + 1 <= i <= s + 3 and w + 1 <= j <= w + 3)
    ]


def high_low(values):
    high = values.astype(BF16)
    return high, (values - high.astype(F32)).astype(BF16)


def stack_split(rows):
    high = rows.astype(BF16).astype(F32)
    return jnp.concatenate([high, rows - high], 0).astype(BF16)


def split_dot(stacked, matrix, dims):
    high, low = high_low(matrix)
    return lax.dot_general(stacked, high, dims, preferred_element_type=F32) + lax.dot_general(
        stacked, low, dims, preferred_element_type=F32
    )


def fold(rows):
    return rows[0:4] + rows[4:8]


def kernel(
    n_x, n_y, slots,
    vec_h, ord_h, near_h, bas_h, cl_h, tl_h, cn_h, tn_h, td_h, cu_h, pairs_h, pairs_s,
    out_ref,
    vec_v, ord_v, near_v, bas_v, cl_v, tl_v, cn_v, tn_v, td_v, cu_v, pairs_v,
    vs_v, onehot_v, ext, xs_v, nodex, table, tbl2, prod, rs_send, rs_recv, rs1, rs2,
    far_node, far_leaf, near_y, y_v,
    small_sem, near_sem, cl_sem, cn_sem,
    halo_send, halo_recv, ag1_send, ag1_recv, ag2_send, ag2_recv,
    rsa_send, rsa_recv, rsb_send, rsb_recv,
):
    gi, gj = lax.axis_index("gx"), lax.axis_index("gy")

    small = [
        pltpu.make_async_copy(src, dst, small_sem.at[k])
        for k, (src, dst) in enumerate([
            (vec_h, vec_v), (ord_h, ord_v), (bas_h, bas_v), (tl_h, tl_v), (tn_h, tn_v),
            (td_h, td_v), (pairs_h, pairs_v), (cu_h, cu_v),
        ])
    ]
    for copy in small:
        copy.start()
    node_copy = pltpu.make_async_copy(cn_h, cn_v, cn_sem)
    node_copy.start()

    def cl_copy(leaf):
        return pltpu.make_async_copy(cl_h.at[leaf], cl_v.at[leaf], cl_sem.at[leaf])

    def near_copy(leaf):
        return pltpu.make_async_copy(near_h.at[leaf], near_v.at[leaf], near_sem.at[leaf])

    for u in range(2):
        for v in range(2):
            for s in range(2):
                for w in range(2):
                    cl_copy((2 * u + s) * 4 + 2 * v + w).start()
    for leaf in range(16):
        near_copy(leaf).start()

    ext[...] = jnp.zeros_like(ext)

    def inside(dx, dy):
        ok = None
        for pos, step, count in ((gi, dx, n_x), (gj, dy, n_y)):
            if step == 0:
                continue
            here = pos + step < count if step > 0 else pos + step >= 0
            ok = here if ok is None else jnp.logical_and(ok, here)
        return ok

    barrier = pltpu.get_barrier_semaphore()
    for k in range(1, n_x):
        pl.semaphore_signal(barrier, inc=1, device_id=(lax.rem(gi + k, n_x), gj), device_id_type=MESH)
    for k in range(1, n_y):
        pl.semaphore_signal(barrier, inc=1, device_id=(gi, lax.rem(gj + k, n_y)), device_id_type=MESH)
    diagonal = 0
    for dx, dy in DIRECTIONS:
        if dx != 0 and dy != 0:
            ok = inside(dx, dy)
            diagonal = diagonal + ok.astype(jnp.int32)

            @pl.when(ok)
            def _(dx=dx, dy=dy):
                pl.semaphore_signal(barrier, inc=1, device_id=(gi + dx, gj + dy), device_id_type=MESH)

    small[0].wait()
    small[1].wait()
    vec = vec_v[...]
    vec_high = vec.astype(BF16).astype(F32)
    vec_low = vec - vec_high
    for kh in range(16):
        cols = slice(kh * 128, kh * 128 + 128)
        vs_v[kh * 8 : kh * 8 + 4, :] = vec_high[:, cols]
        vs_v[kh * 8 + 4 : kh * 8 + 8, :] = vec_low[:, cols]
    order = ord_v[...]
    order_low = jnp.bitwise_and(order, 127)
    order_high = lax.shift_right_logical(order, 7)
    sub = lax.broadcasted_iota(jnp.int32, (128, 128), 0)
    row_group = lax.shift_right_logical(sub, 3)
    vs = vs_v[...].astype(BF16)
    small[2].wait()
    for leaf in range(16):
        cols = slice(leaf * 128, leaf * 128 + 128)
        onehot = jnp.where(sub == order_low[:, cols], 1.0, 0.0).astype(BF16)
        onehot_v[:, cols] = onehot
        picked = lax.dot_general(vs, onehot, NN, preferred_element_type=F32)
        picked = jnp.where(row_group == order_high[:, cols], picked, 0.0)
        stacked = jnp.sum(picked.reshape(16, 8, 128), axis=0)
        up = fold(split_dot(stacked.astype(BF16), bas_v[leaf], NT))
        a, b = leaf // 4, leaf % 4
        ext[2 + a, 2 + b, 0:4, :] = fold(stacked)
        ext[2 + a, 2 + b, 4:8, 0:64] = up

    small[3].wait()
    small[4].wait()
    small[5].wait()
    up_device = jnp.zeros((8, 64), F32)
    for u in range(2):
        for v in range(2):
            node = jnp.zeros((8, 64), F32)
            for s in range(2):
                for w in range(2):
                    a, b = 2 * u + s, 2 * v + w
                    child = stack_split(ext[2 + a, 2 + b, 4:8, 0:64])
                    node = node + split_dot(child, tl_v[a * 4 + b], NN)
            node = fold(node)
            for p in range(2):
                for q in range(2):
                    ext[2 + 2 * p + u, 2 + 2 * q + v, 4:8, 64:128] = node
            up_device = up_device + split_dot(stack_split(node), tn_v[u * 2 + v], NN)
    up_device = fold(up_device)
    toward = fold(split_dot(stack_split(up_device), td_v[...], NN))
    table[gj, gi] = jnp.concatenate([up_device, toward], 1)

    pl.semaphore_wait(barrier, n_x - 1 + n_y - 1 + diagonal)

    def ag1(to):
        return pltpu.make_async_remote_copy(
            src_ref=table.at[gj, gi], dst_ref=table.at[gj, gi],
            send_sem=ag1_send.at[to], recv_sem=ag1_recv.at[gi],
            device_id=(to, gj), device_id_type=MESH)

    def ag1_in(source):
        return pltpu.make_async_remote_copy(
            src_ref=table.at[gj, gi], dst_ref=table.at[gj, source],
            send_sem=ag1_send.at[source], recv_sem=ag1_recv.at[source],
            device_id=(source, gj), device_id_type=MESH)

    for k in range(1, n_x):
        ag1(lax.rem(gi + k, n_x)).start()

    cut = {-1: (2, 2, 6), 0: (2, 4, 2), 1: (4, 2, 0)}

    def halo(index):
        dx, dy = DIRECTIONS[index]
        (r0, rn, rd), (c0, cn, cd) = cut[dx], cut[dy]
        return pltpu.make_async_remote_copy(
            src_ref=ext.at[r0 : r0 + rn, c0 : c0 + cn], dst_ref=ext.at[rd : rd + rn, cd : cd + cn],
            send_sem=halo_send.at[index], recv_sem=halo_recv.at[index],
            device_id=(gi + dx, gj + dy), device_id_type=MESH)

    for index, (dx, dy) in enumerate(DIRECTIONS):
        @pl.when(inside(dx, dy))
        def _(index=index):
            halo(index).start()

    for k in range(1, n_x):
        ag1_in(lax.rem(gi + k, n_x)).wait_recv()

    def ag2(to):
        return pltpu.make_async_remote_copy(
            src_ref=table.at[gj], dst_ref=table.at[gj],
            send_sem=ag2_send.at[to], recv_sem=ag2_recv.at[gj],
            device_id=(gi, to), device_id_type=MESH)

    def ag2_in(source):
        return pltpu.make_async_remote_copy(
            src_ref=table.at[gj], dst_ref=table.at[source],
            send_sem=ag2_send.at[source], recv_sem=ag2_recv.at[source],
            device_id=(gi, source), device_id_type=MESH)

    for k in range(1, n_y):
        ag2(lax.rem(gj + k, n_y)).start()

    for index, (dx, dy) in enumerate(DIRECTIONS):
        @pl.when(inside(dx, dy))
        def _(dx=dx, dy=dy):
            halo(DIRECTIONS.index((-dx, -dy))).wait_recv()

    for r in range(6):
        for c in range(6):
            x = ext[r + 1, c + 1, 0:4, :]
            high = x.astype(BF16).astype(F32)
            xs_v[r, c, 0:4, :] = high
            xs_v[r, c, 4:8, :] = x - high
            tile_r, tile_c = (0, 2, 6)[r // 2] + r % 2, (0, 2, 6)[c // 2] + c % 2
            nodex[r, c, 0:4, :] = pltpu.roll(ext[tile_r, tile_c], 64, 1)[4:8]

    row8 = lax.broadcasted_iota(jnp.int32, (8, 64), 0)
    pick_row = [jnp.where(row8 == n, 1.0, 0.0).astype(BF16) for n in range(4)]

    def far_sum(blocks, source):
        acc = [jnp.zeros((64, 64), F32) for _ in range(4)]
        for g in range(27):
            block = blocks(g)
            for n in range(4):
                acc[n] = acc[n] + block * source(g, n)
        total = jnp.zeros((8, 64), F32)
        for n in range(4):
            for part in high_low(acc[n]):
                total = total + lax.dot_general(pick_row[n], part, NT, preferred_element_type=F32)
        return total

    def far_leaf_group(u, v):
        for s in range(2):
            for w in range(2):
                layout = slots_of(s, w)
                leaf = (2 * u + s) * 4 + 2 * v + w
                cl_copy(leaf).wait()
                far_leaf[leaf] = far_sum(
                    lambda g: cl_v[leaf, g],
                    lambda g, n: ext[2 * u + layout[g][0], 2 * v + layout[g][1], 4 + n : 5 + n, 0:64],
                )

    def far_node_group(box, s, w):
        layout = slots_of(s, w)
        far_node[box] = far_sum(
            lambda g: cn_v[box, g],
            lambda g, n: nodex[layout[g][0], layout[g][1], n : n + 1, 0:64],
        )

    def near_leaf(leaf):
        a, b = lax.div(leaf, 4), lax.rem(leaf, 4)
        near_copy(leaf).wait()
        total = jnp.zeros((8, 128), F32)
        for e in range(9):
            stacked = xs_v[a + e // 3, b + e % 3].astype(BF16)
            total = total + split_dot(stacked, near_v[leaf, e], NT)
        near_y[leaf] = total

    def loop(low, high, body):
        lax.fori_loop(low, high, lambda k, c: (body(k), c)[1], 0)

    node_copy.wait()
    for s in range(2):
        for w in range(2):
            far_node_group(2 * s + w, s, w)
    loop(0, 2, lambda v: far_leaf_group(0, v))

    for k in range(1, n_y):
        ag2_in(lax.rem(gj + k, n_y)).wait_recv()

    devices = n_x * n_y
    full = table[...]
    groups = full.reshape(n_y // 2, 2, n_x // 2, 2, 4, 128).sum(axis=(1, 3)).reshape(devices // 4, 4, 128)
    full = full.reshape(devices, 4, 128)
    high = full.astype(BF16).astype(F32)
    tbl2[0:devices, 0:4, :] = high
    tbl2[0:devices, 4:8, :] = full - high
    high = groups.astype(BF16).astype(F32)
    tbl2[devices:, 0:4, :] = pltpu.roll(high, 64, 2)
    tbl2[devices:, 4:8, :] = pltpu.roll(groups - high, 64, 2)

    small[6].wait()
    small[7].wait()
    prod[...] = jnp.zeros_like(prod)
    for k in range(slots):
        source = pairs_s[1, 0, k]
        group = source - devices
        place = jnp.where(
            source < devices,
            lax.rem(source, n_y) * n_x + lax.div(source, n_y),
            devices + lax.rem(group, n_y // 2) * (n_x // 2) + lax.div(group, n_y // 2),
        )
        stacked = tbl2[place, :, 0:64].astype(BF16)
        prod[k * 8 : k * 8 + 4, 0:64] = fold(split_dot(stacked, cu_v[k], NT))

    target = pairs_v[0]
    row = lax.broadcasted_iota(jnp.int32, (devices, slots), 0)
    row_j, row_i = lax.div(row, n_x), lax.rem(row, n_x)
    own_box = row_i * n_y + row_j
    parent_box = devices + lax.div(row_i, 2) * (n_y // 2) + lax.div(row_j, 2)
    pick_own = jnp.where(own_box == target, 1.0, 0.0).astype(BF16)
    pick_parent = jnp.where(parent_box == target, 1.0, 0.0).astype(BF16)
    for n in range(4):
        rows = prod[pl.ds(n, 40, stride=8), :][0:slots, 0:64]
        sums = []
        for pick in (pick_own, pick_parent):
            part = 0.0
            for piece in high_low(rows):
                part = part + lax.dot_general(pick, piece, NN, preferred_element_type=F32)
            sums.append(part)
        both = jnp.concatenate(sums, 1)
        rs_send[:, :, n : n + 1, :] = both.reshape(n_y, n_x, 1, 128)

    def rsa(to):
        return pltpu.make_async_remote_copy(
            src_ref=rs_send.at[to], dst_ref=rs_recv.at[gj],
            send_sem=rsa_send.at[to], recv_sem=rsa_recv.at[gj],
            device_id=(gi, to), device_id_type=MESH)

    def rsa_in(source):
        return pltpu.make_async_remote_copy(
            src_ref=rs_send.at[source], dst_ref=rs_recv.at[source],
            send_sem=rsa_send.at[source], recv_sem=rsa_recv.at[source],
            device_id=(gi, source), device_id_type=MESH)

    for k in range(1, n_y):
        rsa(lax.rem(gj + k, n_y)).start()
    rs_recv[gj] = rs_send[gj]

    loop(0, 2, lambda v: far_leaf_group(1, v))
    loop(0, 4, near_leaf)

    for k in range(1, n_y):
        rsa_in(lax.rem(gj + k, n_y)).wait_recv()
    rs1[...] = jnp.sum(rs_recv[...], axis=0)

    def rsb(to):
        return pltpu.make_async_remote_copy(
            src_ref=rs1.at[to], dst_ref=rs2.at[gi],
            send_sem=rsb_send.at[to], recv_sem=rsb_recv.at[gi],
            device_id=(to, gj), device_id_type=MESH)

    def rsb_in(source):
        return pltpu.make_async_remote_copy(
            src_ref=rs1.at[source], dst_ref=rs2.at[source],
            send_sem=rsb_send.at[source], recv_sem=rsb_recv.at[source],
            device_id=(source, gj), device_id_type=MESH)

    for k in range(1, n_x):
        rsb(lax.rem(gi + k, n_x)).start()
    rs2[gi] = rs1[gi]

    loop(4, 16, near_leaf)

    for k in range(1, n_x):
        rsb_in(lax.rem(gi + k, n_x)).wait_recv()
    sums = jnp.sum(rs2[...], axis=0)

    down_device = sums[:, 0:64] + fold(split_dot(stack_split(sums[:, 64:128]), td_v[...], NT))
    device_rows = stack_split(down_device)
    for u in range(2):
        for v in range(2):
            box = u * 2 + v
            down_node = far_node[box][0:4] + fold(split_dot(device_rows, tn_v[box], NT))
            node_rows = stack_split(down_node)
            for s in range(2):
                for w in range(2):
                    leaf = (2 * u + s) * 4 + 2 * v + w
                    down_leaf = far_leaf[leaf][0:4] + fold(split_dot(node_rows, tl_v[leaf], NT))
                    y = split_dot(stack_split(down_leaf), bas_v[leaf], NN) + near_y[leaf]
                    y_v[:, leaf * 128 : leaf * 128 + 128] = stack_split(fold(y)).astype(F32)

    total = jnp.zeros((128, 128), F32)
    for leaf in range(16):
        cols = slice(leaf * 128, leaf * 128 + 128)
        y = y_v[:, cols]
        spread = jnp.broadcast_to(y[None], (16, 8, 128)).reshape(128, 128)
        spread = jnp.where(row_group == order_high[:, cols], spread, 0.0).astype(BF16)
        total = total + lax.dot_general(spread, onehot_v[:, cols], NT, preferred_element_type=F32)
    for kh in range(16):
        out_ref[:, kh * 128 : kh * 128 + 128] = fold(total[kh * 8 : kh * 8 + 8])

    for k in range(1, n_x):
        ag1(lax.rem(gi + k, n_x)).wait_send()
        rsb(lax.rem(gi + k, n_x)).wait_send()
    for k in range(1, n_y):
        ag2(lax.rem(gj + k, n_y)).wait_send()
        rsa(lax.rem(gj + k, n_y)).wait_send()
    for index, (dx, dy) in enumerate(DIRECTIONS):
        @pl.when(inside(dx, dy))
        def _(index=index):
            halo(index).wait_send()


def on_device(
    n_x, n_y,
    vectors, cluster_order, near_blocks, leaf_basis, couple_leaf, transfer_leaf,
    couple_node, transfer_node, transfer_device, couple_upper, pair_list,
):
    slots = couple_upper.shape[1]
    devices = n_x * n_y
    near = near_blocks.transpose(0, 1, 3, 2, 4).reshape(16, 9, 128, 128)
    basis = leaf_basis.transpose(0, 1, 3, 2).reshape(16, 64, 128)
    cl = couple_leaf.transpose(0, 1, 3, 2, 4).reshape(16, 27, 64, 64)
    cn = couple_node.transpose(0, 1, 3, 2, 4).reshape(4, 27, 64, 64)
    tl = transfer_leaf.reshape(16, 64, 64)
    tn = transfer_node.reshape(4, 64, 64)
    td = transfer_device.reshape(64, 64)
    cu = couple_upper.reshape(slots, 64, 64)
    dma = pltpu.SemaphoreType.DMA
    any_spec = pl.BlockSpec(memory_space=pl.ANY)
    return pl.pallas_call(
        functools.partial(kernel, n_x, n_y, slots),
        out_shape=jax.ShapeDtypeStruct((4, 2048), F32),
        in_specs=[any_spec] * 11 + [pl.BlockSpec(memory_space=pltpu.SMEM)],
        out_specs=pl.BlockSpec(memory_space=pltpu.VMEM),
        scratch_shapes=[
            pltpu.VMEM((4, 2048), F32),
            pltpu.VMEM((1, 2048), jnp.int32),
            pltpu.VMEM((16, 9, 128, 128), F32),
            pltpu.VMEM((16, 64, 128), F32),
            pltpu.VMEM((16, 27, 64, 64), F32),
            pltpu.VMEM((16, 64, 64), F32),
            pltpu.VMEM((4, 27, 64, 64), F32),
            pltpu.VMEM((4, 64, 64), F32),
            pltpu.VMEM((64, 64), F32),
            pltpu.VMEM((slots, 64, 64), F32),
            pltpu.VMEM((2, 1, slots), jnp.int32),
            pltpu.VMEM((128, 128), F32),
            pltpu.VMEM((128, 2048), BF16),
            pltpu.VMEM((8, 8, 8, 128), F32),
            pltpu.VMEM((6, 6, 8, 128), F32),
            pltpu.VMEM((6, 6, 8, 128), F32),
            pltpu.VMEM((n_y, n_x, 4, 128), F32),
            pltpu.VMEM((devices + devices // 4, 8, 128), F32),
            pltpu.VMEM((320, 128), F32),
            pltpu.VMEM((n_y, n_x, 4, 128), F32),
            pltpu.VMEM((n_y, n_x, 4, 128), F32),
            pltpu.VMEM((n_x, 4, 128), F32),
            pltpu.VMEM((n_x, 4, 128), F32),
            pltpu.VMEM((4, 8, 64), F32),
            pltpu.VMEM((16, 8, 64), F32),
            pltpu.VMEM((16, 8, 128), F32),
            pltpu.VMEM((8, 2048), F32),
            dma((8,)), dma((16,)), dma((16,)), dma(()),
            dma((8,)), dma((8,)), dma((n_x,)), dma((n_x,)), dma((n_y,)), dma((n_y,)),
            dma((n_y,)), dma((n_y,)), dma((n_x,)), dma((n_x,)),
        ],
        compiler_params=pltpu.CompilerParams(
            collective_id=0, has_side_effects=True, vmem_limit_bytes=56 * 1024 * 1024
        ),
    )(vectors, cluster_order, near, basis, cl, tl, cn, tn, td, cu, pair_list, pair_list)


def solution(mesh):
    in_specs = (
        P(None, ("gx", "gy")),
        P(("gx", "gy"), None),
        P("gx", "gy", None, None, None),
        P("gx", "gy", None, None),
        P("gx", "gy", None, None, None),
        P("gx", "gy", None, None),
        P("gx", "gy", None, None, None),
        P("gx", "gy", None, None),
        P("gx", "gy", None, None),
        P(("gx", "gy"), None, None, None),
        P(None, ("gx", "gy"), None),
    )
    out_specs = P(None, ("gx", "gy"))
    return jax.shard_map(
        functools.partial(on_device, mesh.shape["gx"], mesh.shape["gy"]),
        mesh=mesh, in_specs=in_specs, out_specs=out_specs, check_vma=False,
    )
```

```python
import functools

import jax
import jax.numpy as jnp
from jax import lax
from jax.experimental import pallas as pl
from jax.experimental.pallas import tpu as pltpu
from jax.sharding import PartitionSpec as P

F32 = jnp.float32
BF16 = jnp.bfloat16
MESH = pl.DeviceIdType.MESH
NT = (((1,), (1,)), ((), ()))
NN = (((1,), (0,)), ((), ()))
TN = (((0,), (0,)), ((), ()))
DIRECTIONS = [(dx, dy) for dx in (-1, 0, 1) for dy in (-1, 0, 1) if (dx, dy) != (0, 0)]


HOPS = (0, 1, 2, 1)
OFFSETS = sorted(
    [
        (x, y, z, c)
        for c in range(2)
        for x in range(4)
        for y in range(4)
        for z in range(4)
        if (x, y, z, c) != (0, 0, 0, 0)
    ],
    key=lambda o: -(HOPS[o[0]] + HOPS[o[1]] + HOPS[o[2]]),
)


def slots_of(s, w):
    return [
        (i, j)
        for i in range(6)
        for j in range(6)
        if not (s + 1 <= i <= s + 3 and w + 1 <= j <= w + 3)
    ]


def high_low(values):
    high = values.astype(BF16)
    return high, (values - high.astype(F32)).astype(BF16)


def stack_split(rows):
    high = rows.astype(BF16).astype(F32)
    return jnp.concatenate([high, rows - high], 0).astype(BF16)


def split_dot(stacked, matrix, dims):
    high, low = high_low(matrix)
    return lax.dot_general(stacked, high, dims, preferred_element_type=F32) + lax.dot_general(
        stacked, low, dims, preferred_element_type=F32
    )


def full_dot(left, matrix, dims):
    left_high, left_low = high_low(left)
    high, low = high_low(matrix)
    total = lax.dot_general(left_high, high, dims, preferred_element_type=F32)
    total = total + lax.dot_general(left_low, high, dims, preferred_element_type=F32)
    return total + lax.dot_general(left_high, low, dims, preferred_element_type=F32)


def fold(rows):
    return rows[0:4] + rows[4:8]


def kernel(
    n_x, n_y, slots,
    vec_h, ord_h, near_h, bas_h, cl_h, tl_h, cn_h, tn_h, td_h, cu_h, pairs_h, pairs_s,
    out_ref,
    vec_v, ord_v, near_v, bas_v, cl_v, tl_v, cn_v, tn_v, td_v, cu_v, pairs_v,
    vs_v, onehot_v, ext, xs_v, nodex, mine, table, tbl2, prod, rs_send, rs_recv,
    far_node, near_y, y_v, g_v, w_high, w_low,
    small_sem, near_sem, cl_sem, cn_sem,
    halo_send, halo_recv, ag_send, ag_recv, rs_sent, rs_got,
):
    gi, gj = lax.axis_index("gx"), lax.axis_index("gy")
    devices = n_x * n_y
    me = gi * n_y + gj
    px, core, pz, py = lax.div(gi, 2), lax.rem(gi, 2), lax.div(gj, 4), lax.rem(gj, 4)
    others = []
    for dx, dy, dz, dc in OFFSETS:
        to_i = lax.rem(px + dx, 4) * 2 + lax.rem(core + dc, 2)
        to_j = lax.rem(pz + dz, 4) * 4 + lax.rem(py + dy, 4)
        others.append((to_i, to_j))

    small = [
        pltpu.make_async_copy(src, dst, small_sem.at[k])
        for k, (src, dst) in enumerate([
            (vec_h, vec_v), (ord_h, ord_v), (bas_h, bas_v), (tl_h, tl_v), (tn_h, tn_v),
            (td_h, td_v), (pairs_h, pairs_v), (cu_h, cu_v),
        ])
    ]
    for copy in small:
        copy.start()

    ext[...] = jnp.zeros_like(ext)

    barrier = pltpu.get_barrier_semaphore()
    for other in others:
        pl.semaphore_signal(barrier, inc=1, device_id=other, device_id_type=MESH)

    node_copy = pltpu.make_async_copy(cn_h, cn_v, cn_sem)

    def cl_copy(leaf):
        return pltpu.make_async_copy(cl_h.at[leaf], cl_v.at[leaf], cl_sem.at[leaf])

    def near_copy(leaf):
        return pltpu.make_async_copy(near_h.at[leaf], near_v.at[leaf], near_sem.at[leaf])

    def start_cl(u):
        for v in range(2):
            for s in range(2):
                for w in range(2):
                    cl_copy((2 * u + s) * 4 + 2 * v + w).start()

    for leaf in range(16):
        near_copy(leaf).start()
    node_copy.start()
    start_cl(0)

    def inside(dx, dy):
        ok = None
        for pos, step, count in ((gi, dx, n_x), (gj, dy, n_y)):
            if step == 0:
                continue
            here = pos + step < count if step > 0 else pos + step >= 0
            ok = here if ok is None else jnp.logical_and(ok, here)
        return ok

    small[0].wait()
    small[1].wait()
    vec = vec_v[...]
    vec_high = vec.astype(BF16).astype(F32)
    vec_low = vec - vec_high
    for kh in range(16):
        cols = slice(kh * 128, kh * 128 + 128)
        vs_v[kh * 8 : kh * 8 + 4, :] = vec_high[:, cols]
        vs_v[kh * 8 + 4 : kh * 8 + 8, :] = vec_low[:, cols]
    order = ord_v[...]
    order_low = jnp.bitwise_and(order, 127)
    order_high = lax.shift_right_logical(order, 7)
    sub = lax.broadcasted_iota(jnp.int32, (128, 128), 0)
    row_group = lax.shift_right_logical(sub, 3)
    vs = vs_v[...].astype(BF16)
    small[2].wait()
    for leaf in range(16):
        cols = slice(leaf * 128, leaf * 128 + 128)
        onehot = jnp.where(sub == order_low[:, cols], 1.0, 0.0).astype(BF16)
        onehot_v[:, cols] = onehot
        picked = lax.dot_general(vs, onehot, NN, preferred_element_type=F32)
        picked = jnp.where(row_group == order_high[:, cols], picked, 0.0)
        stacked = jnp.sum(picked.reshape(16, 8, 128), axis=0)
        up = fold(split_dot(stacked.astype(BF16), bas_v[leaf], NT))
        a, b = leaf // 4, leaf % 4
        ext[2 + a, 2 + b, 0:4, :] = fold(stacked)
        ext[2 + a, 2 + b, 4:8, 0:64] = up
        xs_v[1 + a, 1 + b] = stacked

    small[3].wait()
    small[4].wait()
    small[5].wait()
    up_device = jnp.zeros((8, 64), F32)
    for u in range(2):
        for v in range(2):
            node = jnp.zeros((8, 64), F32)
            for s in range(2):
                for w in range(2):
                    a, b = 2 * u + s, 2 * v + w
                    child = stack_split(ext[2 + a, 2 + b, 4:8, 0:64])
                    node = node + split_dot(child, tl_v[a * 4 + b], NN)
            node = fold(node)
            for p in range(2):
                for q in range(2):
                    ext[2 + 2 * p + u, 2 + 2 * q + v, 4:8, 64:128] = node
            up_device = up_device + split_dot(stack_split(node), tn_v[u * 2 + v], NN)
    up_device = fold(up_device)
    toward = fold(split_dot(stack_split(up_device), td_v[...], NN))
    mine[...] = jnp.concatenate([up_device, toward], 1)
    table[me] = mine[...]

    def near_sum(leaf, wanted):
        a, b = leaf // 4, leaf % 4
        rows, blocks = [], []
        for e in range(9):
            r, c = a + e // 3 - 1, b + e % 3 - 1
            if (0 <= r < 4 and 0 <= c < 4) == wanted:
                rows.append(xs_v[1 + r, 1 + c].astype(BF16))
                blocks.append(jnp.concatenate(high_low(near_v[leaf, e]), 0))
        if not rows:
            return jnp.zeros((8, 128), F32)
        both = lax.dot_general(
            jnp.concatenate(rows, 1), jnp.concatenate(blocks, 1), NT, preferred_element_type=F32
        )
        return both[:, 0:128] + both[:, 128:256]

    for leaf in range(16):
        near_copy(leaf).wait()
        near_y[leaf] = near_sum(leaf, True)

    pl.semaphore_wait(barrier, devices - 1)

    for to in others:
        pltpu.make_async_remote_copy(
            src_ref=mine, dst_ref=table.at[me], send_sem=ag_send, recv_sem=ag_recv,
            device_id=to, device_id_type=MESH).start()

    cut = {-1: (2, 2, 6), 0: (2, 4, 2), 1: (4, 2, 0)}

    def halo(index):
        dx, dy = DIRECTIONS[index]
        (r0, rn, rd), (c0, cn, cd) = cut[dx], cut[dy]
        return pltpu.make_async_remote_copy(
            src_ref=ext.at[r0 : r0 + rn, c0 : c0 + cn], dst_ref=ext.at[rd : rd + rn, cd : cd + cn],
            send_sem=halo_send.at[index], recv_sem=halo_recv.at[index],
            device_id=(gi + dx, gj + dy), device_id_type=MESH)

    for index, (dx, dy) in enumerate(DIRECTIONS):
        @pl.when(inside(dx, dy))
        def _(index=index):
            halo(index).start()

    start_cl(1)

    for u in range(2):
        for v in range(2):
            for s in range(2):
                for w in range(2):
                    leaf = (2 * u + s) * 4 + 2 * v + w
                    cols = slice(leaf * 128, leaf * 128 + 128)
                    step = full_dot(tl_v[leaf], bas_v[leaf], TN)
                    g_v[leaf] = step
                    step = full_dot(tn_v[u * 2 + v], step, TN)
                    high, low = high_low(step)
                    w_high[0:64, cols] = high
                    w_low[0:64, cols] = low
                    step = full_dot(td_v[...], step, TN)
                    high, low = high_low(step)
                    w_high[64:128, cols] = high
                    w_low[64:128, cols] = low

    for index, (dx, dy) in enumerate(DIRECTIONS):
        @pl.when(inside(dx, dy))
        def _(dx=dx, dy=dy):
            halo(DIRECTIONS.index((-dx, -dy))).wait_recv()

    for r in range(6):
        for c in range(6):
            if not (1 <= r <= 4 and 1 <= c <= 4):
                x = ext[r + 1, c + 1, 0:4, :]
                high = x.astype(BF16).astype(F32)
                xs_v[r, c, 0:4, :] = high
                xs_v[r, c, 4:8, :] = x - high
            tile_r, tile_c = (0, 2, 6)[r // 2] + r % 2, (0, 2, 6)[c // 2] + c % 2
            nodex[r, c, 0:4, :] = pltpu.roll(ext[tile_r, tile_c], 64, 1)[4:8]

    row8 = lax.broadcasted_iota(jnp.int32, (8, 64), 0)
    pick_row = [jnp.where(row8 == n, 1.0, 0.0).astype(BF16) for n in range(4)]

    def far_sum(blocks, source):
        acc = [jnp.zeros((64, 64), F32) for _ in range(4)]
        for g in range(27):
            block = blocks(g)
            for n in range(4):
                acc[n] = acc[n] + block * source(g, n)
        total = jnp.zeros((8, 64), F32)
        for n in range(4):
            for part in high_low(acc[n]):
                total = total + lax.dot_general(pick_row[n], part, NT, preferred_element_type=F32)
        return total[0:4]

    def far_leaf_group(u, v):
        node_rows = stack_split(far_node[2 * u + v, 0:4])
        for s in range(2):
            for w in range(2):
                layout = slots_of(s, w)
                leaf = (2 * u + s) * 4 + 2 * v + w
                cl_copy(leaf).wait()
                far = far_sum(
                    lambda g: cl_v[leaf, g],
                    lambda g, n: ext[2 * u + layout[g][0], 2 * v + layout[g][1], 4 + n : 5 + n, 0:64],
                )
                y = split_dot(stack_split(far), bas_v[leaf], NN)
                y = y + split_dot(node_rows, g_v[leaf], NN)
                near_y[leaf] = near_y[leaf] + y

    def far_node_group(box, s, w):
        layout = slots_of(s, w)
        far_node[box, 0:4] = far_sum(
            lambda g: cn_v[box, g],
            lambda g, n: nodex[layout[g][0], layout[g][1], n : n + 1, 0:64],
        )

    def loop(low, high, body):
        lax.fori_loop(low, high, lambda k, c: (body(k), c)[1], 0)

    node_copy.wait()
    for s in range(2):
        for w in range(2):
            far_node_group(2 * s + w, s, w)
    for leaf in range(16):
        if leaf not in (5, 6, 9, 10):
            near_y[leaf] = near_y[leaf] + near_sum(leaf, False)
    loop(0, 1, lambda v: far_leaf_group(0, v))

    most = pl.ds(0, devices - 1)

    def all_but_one(buffer, sent, got):
        return pltpu.make_async_remote_copy(
            src_ref=buffer.at[most], dst_ref=buffer.at[most], send_sem=sent, recv_sem=got,
            device_id=others[0], device_id_type=MESH)

    all_but_one(table, ag_send, ag_recv).wait_recv()

    full = table[...]
    groups = full.reshape(n_x // 2, 2, n_y // 2, 2, 4, 128).sum(axis=(1, 3)).reshape(devices // 4, 4, 128)
    high = full.astype(BF16).astype(F32)
    tbl2[0:devices, 0:4, :] = high
    tbl2[0:devices, 4:8, :] = full - high
    high = groups.astype(BF16).astype(F32)
    tbl2[devices:, 0:4, :] = pltpu.roll(high, 64, 2)
    tbl2[devices:, 4:8, :] = pltpu.roll(groups - high, 64, 2)

    small[6].wait()
    small[7].wait()
    for k in range(slots):
        stacked = tbl2[pairs_s[1, 0, k], :, 0:64].astype(BF16)
        prod[k * 8 : k * 8 + 4, 0:64] = fold(split_dot(stacked, cu_v[k], NT))

    target = pairs_v[0]
    row = lax.broadcasted_iota(jnp.int32, (devices, slots), 0)
    row_i, row_j = lax.div(row, n_y), lax.rem(row, n_y)
    parent_box = devices + lax.div(row_i, 2) * (n_y // 2) + lax.div(row_j, 2)
    pick_own = jnp.where(row == target, 1.0, 0.0).astype(BF16)
    pick_parent = jnp.where(parent_box == target, 1.0, 0.0).astype(BF16)
    for n in range(4):
        rows = prod[pl.ds(n, 40, stride=8), :][0:slots, 0:64]
        sums = []
        for pick in (pick_own, pick_parent):
            part = 0.0
            for piece in high_low(rows):
                part = part + lax.dot_general(pick, piece, NN, preferred_element_type=F32)
            sums.append(part)
        both = jnp.concatenate(sums, 1)
        rs_send[:, n : n + 1, :] = both.reshape(devices, 1, 128)

    for to_i, to_j in others:
        pltpu.make_async_remote_copy(
            src_ref=rs_send.at[to_i * n_y + to_j], dst_ref=rs_recv.at[me],
            send_sem=rs_sent, recv_sem=rs_got,
            device_id=(to_i, to_j), device_id_type=MESH).start()
    rs_recv[me] = rs_send[me]

    loop(1, 2, lambda v: far_leaf_group(0, v))
    loop(0, 2, lambda v: far_leaf_group(1, v))

    all_but_one(rs_recv, rs_sent, rs_got).wait_recv()
    sums = stack_split(jnp.sum(rs_recv[...], axis=0))

    down = lax.dot_general(sums, w_high[...], NN, preferred_element_type=F32)
    down = down + lax.dot_general(sums, w_low[...], NN, preferred_element_type=F32)
    for leaf in range(16):
        cols = slice(leaf * 128, leaf * 128 + 128)
        y_v[:, cols] = stack_split(fold(near_y[leaf] + down[:, cols])).astype(F32)

    total = jnp.zeros((128, 128), F32)
    for leaf in range(16):
        cols = slice(leaf * 128, leaf * 128 + 128)
        y = y_v[:, cols]
        spread = jnp.broadcast_to(y[None], (16, 8, 128)).reshape(128, 128)
        spread = jnp.where(row_group == order_high[:, cols], spread, 0.0).astype(BF16)
        total = total + lax.dot_general(spread, onehot_v[:, cols], NT, preferred_element_type=F32)
    for kh in range(16):
        out_ref[:, kh * 128 : kh * 128 + 128] = fold(total[kh * 8 : kh * 8 + 8])

    all_but_one(table, ag_send, ag_recv).wait_send()
    all_but_one(rs_send, rs_sent, rs_got).wait_send()
    for index, (dx, dy) in enumerate(DIRECTIONS):
        @pl.when(inside(dx, dy))
        def _(index=index):
            halo(index).wait_send()


def on_device(
    n_x, n_y,
    vectors, cluster_order, near_blocks, leaf_basis, couple_leaf, transfer_leaf,
    couple_node, transfer_node, transfer_device, couple_upper, pair_list,
):
    slots = couple_upper.shape[1]
    devices = n_x * n_y
    near = near_blocks.transpose(0, 1, 3, 2, 4).reshape(16, 9, 128, 128)
    basis = leaf_basis.transpose(0, 1, 3, 2).reshape(16, 64, 128)
    cl = couple_leaf.transpose(0, 1, 3, 2, 4).reshape(16, 27, 64, 64)
    cn = couple_node.transpose(0, 1, 3, 2, 4).reshape(4, 27, 64, 64)
    tl = transfer_leaf.reshape(16, 64, 64)
    tn = transfer_node.reshape(4, 64, 64)
    td = transfer_device.reshape(64, 64)
    cu = couple_upper.reshape(slots, 64, 64)
    dma = pltpu.SemaphoreType.DMA
    any_spec = pl.BlockSpec(memory_space=pl.ANY)
    return pl.pallas_call(
        functools.partial(kernel, n_x, n_y, slots),
        out_shape=jax.ShapeDtypeStruct((4, 2048), F32),
        in_specs=[any_spec] * 11 + [pl.BlockSpec(memory_space=pltpu.SMEM)],
        out_specs=pl.BlockSpec(memory_space=pltpu.VMEM),
        scratch_shapes=[
            pltpu.VMEM((4, 2048), F32),
            pltpu.VMEM((1, 2048), jnp.int32),
            pltpu.VMEM((16, 9, 128, 128), F32),
            pltpu.VMEM((16, 64, 128), F32),
            pltpu.VMEM((16, 27, 64, 64), F32),
            pltpu.VMEM((16, 64, 64), F32),
            pltpu.VMEM((4, 27, 64, 64), F32),
            pltpu.VMEM((4, 64, 64), F32),
            pltpu.VMEM((64, 64), F32),
            pltpu.VMEM((slots, 64, 64), F32),
            pltpu.VMEM((2, 1, slots), jnp.int32),
            pltpu.VMEM((128, 128), F32),
            pltpu.VMEM((128, 2048), BF16),
            pltpu.VMEM((8, 8, 8, 128), F32),
            pltpu.VMEM((6, 6, 8, 128), F32),
            pltpu.VMEM((6, 6, 8, 128), F32),
            pltpu.VMEM((4, 128), F32),
            pltpu.VMEM((devices, 4, 128), F32),
            pltpu.VMEM((devices + devices // 4, 8, 128), F32),
            pltpu.VMEM((320, 128), F32),
            pltpu.VMEM((devices, 4, 128), F32),
            pltpu.VMEM((devices, 4, 128), F32),
            pltpu.VMEM((4, 8, 64), F32),
            pltpu.VMEM((16, 8, 128), F32),
            pltpu.VMEM((8, 2048), F32),
            pltpu.VMEM((16, 64, 128), F32),
            pltpu.VMEM((128, 2048), BF16),
            pltpu.VMEM((128, 2048), BF16),
            dma((8,)), dma((16,)), dma((16,)), dma(()),
            dma((8,)), dma((8,)), dma(()), dma(()), dma(()), dma(()),
        ],
        compiler_params=pltpu.CompilerParams(
            collective_id=0, has_side_effects=True, vmem_limit_bytes=56 * 1024 * 1024
        ),
    )(vectors, cluster_order, near, basis, cl, tl, cn, tn, td, cu, pair_list, pair_list)


def solution(mesh):
    in_specs = (
        P(None, ("gx", "gy")),
        P(("gx", "gy"), None),
        P("gx", "gy", None, None, None),
        P("gx", "gy", None, None),
        P("gx", "gy", None, None, None),
        P("gx", "gy", None, None),
        P("gx", "gy", None, None, None),
        P("gx", "gy", None, None),
        P("gx", "gy", None, None),
        P(("gx", "gy"), None, None, None),
        P(None, ("gx", "gy"), None),
    )
    out_specs = P(None, ("gx", "gy"))
    return jax.shard_map(
        functools.partial(on_device, mesh.shape["gx"], mesh.shape["gy"]),
        mesh=mesh, in_specs=in_specs, out_specs=out_specs, check_vma=False,
    )
```

```python
import functools

import jax
import jax.numpy as jnp
from jax import lax
from jax.experimental import pallas as pl
from jax.experimental.pallas import tpu as pltpu
from jax.sharding import PartitionSpec as P

F32 = jnp.float32
BF16 = jnp.bfloat16
MESH = pl.DeviceIdType.MESH
NT = (((1,), (1,)), ((), ()))
NN = (((1,), (0,)), ((), ()))
TN = (((0,), (0,)), ((), ()))
DIRECTIONS = [(dx, dy) for dx in (-1, 0, 1) for dy in (-1, 0, 1) if (dx, dy) != (0, 0)]


HOPS = (0, 1, 2, 1)
OFFSETS = sorted(
    [
        (x, y, z, c)
        for c in range(2)
        for x in range(4)
        for y in range(4)
        for z in range(4)
        if (x, y, z, c) != (0, 0, 0, 0)
    ],
    key=lambda o: -(HOPS[o[0]] + HOPS[o[1]] + HOPS[o[2]]),
)


def slots_of(s, w):
    return [
        (i, j)
        for i in range(6)
        for j in range(6)
        if not (s + 1 <= i <= s + 3 and w + 1 <= j <= w + 3)
    ]


def high_low(values):
    high = values.astype(BF16)
    return high, (values - high.astype(F32)).astype(BF16)


def stack_split(rows):
    high = rows.astype(BF16).astype(F32)
    return jnp.concatenate([high, rows - high], 0).astype(BF16)


def split_dot(stacked, matrix, dims):
    high, low = high_low(matrix)
    return lax.dot_general(stacked, high, dims, preferred_element_type=F32) + lax.dot_general(
        stacked, low, dims, preferred_element_type=F32
    )


def full_dot(left, matrix, dims):
    left_high, left_low = high_low(left)
    high, low = high_low(matrix)
    total = lax.dot_general(left_high, high, dims, preferred_element_type=F32)
    total = total + lax.dot_general(left_low, high, dims, preferred_element_type=F32)
    return total + lax.dot_general(left_high, low, dims, preferred_element_type=F32)


def fold(rows):
    return rows[0:4] + rows[4:8]


def kernel(
    n_x, n_y, slots,
    vec_h, ord_h, near_h, bas_h, cl_h, tl_h, cn_h, tn_h, td_h, cu_h, pairs_h, pairs_s,
    out_ref,
    vec_v, ord_v, near_v, bas_v, cl_v, tl_v, cn_v, tn_v, td_v, cu_v, pairs_v,
    vs_v, onehot_v, ext, xs_v, leaf_row, leaf_col, node_row, node_col, mine, table, tbl2, prod, rs_send, rs_recv,
    raw_far, near_y, y_v, g_v, w_high, w_low,
    small_sem, near_sem, cl_sem, cn_sem,
    halo_send, halo_recv, ag_send, ag_recv, rs_sent, rs_got,
):
    gi, gj = lax.axis_index("gx"), lax.axis_index("gy")
    devices = n_x * n_y
    me = gi * n_y + gj
    px, core, pz, py = lax.div(gi, 2), lax.rem(gi, 2), lax.div(gj, 4), lax.rem(gj, 4)
    others = []
    for dx, dy, dz, dc in OFFSETS:
        to_i = lax.rem(px + dx, 4) * 2 + lax.rem(core + dc, 2)
        to_j = lax.rem(pz + dz, 4) * 4 + lax.rem(py + dy, 4)
        others.append((to_i, to_j))

    small = [
        pltpu.make_async_copy(src, dst, small_sem.at[k])
        for k, (src, dst) in enumerate([
            (vec_h, vec_v), (ord_h, ord_v), (bas_h, bas_v), (tl_h, tl_v), (tn_h, tn_v),
            (td_h, td_v), (pairs_h, pairs_v), (cu_h, cu_v),
        ])
    ]
    for copy in small:
        copy.start()

    ext[...] = jnp.zeros_like(ext)

    barrier = pltpu.get_barrier_semaphore()
    for other in others:
        pl.semaphore_signal(barrier, inc=1, device_id=other, device_id_type=MESH)

    node_copy = pltpu.make_async_copy(cn_h, cn_v, cn_sem)

    def cl_copy(leaf):
        return pltpu.make_async_copy(cl_h.at[leaf], cl_v.at[leaf], cl_sem.at[leaf])

    def near_copy(leaf):
        return pltpu.make_async_copy(near_h.at[leaf], near_v.at[leaf], near_sem.at[leaf])

    def start_cl(u):
        for v in range(2):
            for s in range(2):
                for w in range(2):
                    cl_copy((2 * u + s) * 4 + 2 * v + w).start()

    for leaf in range(16):
        near_copy(leaf).start()
    node_copy.start()
    start_cl(0)
    start_cl(1)

    def inside(dx, dy):
        ok = None
        for pos, step, count in ((gi, dx, n_x), (gj, dy, n_y)):
            if step == 0:
                continue
            here = pos + step < count if step > 0 else pos + step >= 0
            ok = here if ok is None else jnp.logical_and(ok, here)
        return ok

    small[0].wait()
    small[1].wait()
    vec = vec_v[...]
    vec_high = vec.astype(BF16).astype(F32)
    vec_low = vec - vec_high
    for kh in range(16):
        cols = slice(kh * 128, kh * 128 + 128)
        vs_v[kh * 8 : kh * 8 + 4, :] = vec_high[:, cols]
        vs_v[kh * 8 + 4 : kh * 8 + 8, :] = vec_low[:, cols]
    order = ord_v[...]
    order_low = jnp.bitwise_and(order, 127)
    order_high = lax.shift_right_logical(order, 7)
    sub = lax.broadcasted_iota(jnp.int32, (128, 128), 0)
    row_group = lax.shift_right_logical(sub, 3)
    vs = vs_v[...].astype(BF16)
    small[2].wait()
    for leaf in range(16):
        cols = slice(leaf * 128, leaf * 128 + 128)
        onehot = jnp.where(sub == order_low[:, cols], 1.0, 0.0).astype(BF16)
        onehot_v[:, cols] = onehot
        picked = lax.dot_general(vs, onehot, NN, preferred_element_type=F32)
        picked = jnp.where(row_group == order_high[:, cols], picked, 0.0)
        stacked = jnp.sum(picked.reshape(16, 8, 128), axis=0)
        up = fold(split_dot(stacked.astype(BF16), bas_v[leaf], NT))
        a, b = leaf // 4, leaf % 4
        ext[2 + a, 2 + b, 0:4, :] = fold(stacked)
        ext[2 + a, 2 + b, 4:8, 0:64] = up
        xs_v[1 + a, 1 + b] = stacked

    small[3].wait()
    small[4].wait()
    small[5].wait()
    up_device = jnp.zeros((8, 64), F32)
    for u in range(2):
        for v in range(2):
            node = jnp.zeros((8, 64), F32)
            for s in range(2):
                for w in range(2):
                    a, b = 2 * u + s, 2 * v + w
                    child = stack_split(ext[2 + a, 2 + b, 4:8, 0:64])
                    node = node + split_dot(child, tl_v[a * 4 + b], NN)
            node = fold(node)
            for p in range(2):
                for q in range(2):
                    ext[2 + 2 * p + u, 2 + 2 * q + v, 4:8, 64:128] = node
            up_device = up_device + split_dot(stack_split(node), tn_v[u * 2 + v], NN)
    up_device = fold(up_device)
    toward = fold(split_dot(stack_split(up_device), td_v[...], NN))
    mine[...] = jnp.concatenate([up_device, toward], 1)
    table[me] = mine[...]

    def near_sum(leaf, wanted):
        a, b = leaf // 4, leaf % 4
        rows, blocks = [], []
        for e in range(9):
            r, c = a + e // 3 - 1, b + e % 3 - 1
            if (0 <= r < 4 and 0 <= c < 4) == wanted:
                rows.append(xs_v[1 + r, 1 + c].astype(BF16))
                blocks.append(jnp.concatenate(high_low(near_v[leaf, e]), 0))
        if not rows:
            return jnp.zeros((8, 128), F32)
        both = lax.dot_general(
            jnp.concatenate(rows, 1), jnp.concatenate(blocks, 1), NT, preferred_element_type=F32
        )
        return both[:, 0:128] + both[:, 128:256]

    pl.semaphore_wait(barrier, devices - 1)

    for to in others:
        pltpu.make_async_remote_copy(
            src_ref=mine, dst_ref=table.at[me], send_sem=ag_send, recv_sem=ag_recv,
            device_id=to, device_id_type=MESH).start()

    cut = {-1: (2, 2, 6), 0: (2, 4, 2), 1: (4, 2, 0)}

    def halo(index):
        dx, dy = DIRECTIONS[index]
        (r0, rn, rd), (c0, cn, cd) = cut[dx], cut[dy]
        return pltpu.make_async_remote_copy(
            src_ref=ext.at[r0 : r0 + rn, c0 : c0 + cn], dst_ref=ext.at[rd : rd + rn, cd : cd + cn],
            send_sem=halo_send.at[index], recv_sem=halo_recv.at[index],
            device_id=(gi + dx, gj + dy), device_id_type=MESH)

    for index, (dx, dy) in enumerate(DIRECTIONS):
        @pl.when(inside(dx, dy))
        def _(index=index):
            halo(index).start()

    for leaf in range(16):
        near_copy(leaf).wait()
    for leaf in range(16):
        near_y[leaf] = near_sum(leaf, True)

    small[6].wait()
    target = pairs_v[0]
    row = lax.broadcasted_iota(jnp.int32, (devices, slots), 0)
    row_i, row_j = lax.div(row, n_y), lax.rem(row, n_y)
    parent_box = devices + lax.div(row_i, 2) * (n_y // 2) + lax.div(row_j, 2)
    pick_own = jnp.where(row == target, 1.0, 0.0).astype(BF16)
    pick_parent = jnp.where(parent_box == target, 1.0, 0.0).astype(BF16)

    for u in range(2):
        for v in range(2):
            family = [(2 * u + s) * 4 + 2 * v + w for s in range(2) for w in range(2)]
            steps = [full_dot(tl_v[leaf], bas_v[leaf], TN) for leaf in family]
            for leaf, step in zip(family, steps):
                g_v[leaf] = step
            down = full_dot(tn_v[u * 2 + v], jnp.concatenate(steps, 1), TN)
            both = jnp.concatenate([down, full_dot(td_v[...], down, TN)], 0)
            high, low = high_low(both)
            for k, leaf in enumerate(family):
                cols = slice(leaf * 128, leaf * 128 + 128)
                w_high[:, cols] = high[:, k * 128 : k * 128 + 128]
                w_low[:, cols] = low[:, k * 128 : k * 128 + 128]

    for index, (dx, dy) in enumerate(DIRECTIONS):
        @pl.when(inside(dx, dy))
        def _(dx=dx, dy=dy):
            halo(DIRECTIONS.index((-dx, -dy))).wait_recv()

    for r in range(6):
        for c in range(6):
            if not (1 <= r <= 4 and 1 <= c <= 4):
                x = ext[r + 1, c + 1, 0:4, :]
                high = x.astype(BF16).astype(F32)
                xs_v[r, c, 0:4, :] = high
                xs_v[r, c, 4:8, :] = x - high

    lane = lax.broadcasted_iota(jnp.int32, (8, 128), 1)

    def side_by_side(left, right):
        return jnp.where(lane < 64, left, right)

    node_at = (0, 1, 2, 3, 6, 7)
    for r in range(8):
        for c in range(8):
            swapped = pltpu.roll(ext[r, c], 64, 1)
            if c > 0:
                leaf_row[r, c - 1] = side_by_side(ext[r, c - 1], swapped)
            if r > 0:
                leaf_col[r - 1, c] = side_by_side(ext[r - 1, c], swapped)
    for r in range(6):
        for c in range(6):
            here = ext[node_at[r], node_at[c]]
            swapped = pltpu.roll(here, 64, 1)
            if c < 5:
                node_row[r, c] = side_by_side(swapped, ext[node_at[r], node_at[c + 1]])
            if r < 5:
                node_col[r, c] = side_by_side(swapped, ext[node_at[r + 1], node_at[c]])

    row8 = lax.broadcasted_iota(jnp.int32, (8, 512), 0)
    group8 = lax.shift_right_logical(lax.broadcasted_iota(jnp.int32, (8, 512), 1), 7)
    pick_row = jnp.where(row8 == group8, 1.0, 0.0).astype(BF16)

    def far_sum(s, w, blocks, row_pair, column_pair):
        layout = slots_of(s, w)
        acc = [jnp.zeros((64, 128), F32) for _ in range(4)]

        def add(left, right, source):
            pair = jnp.concatenate([blocks(left), jnp.zeros((64, 64), F32) if right is None else blocks(right)], 1)
            for n in range(4):
                acc[n] = acc[n] + pair * source(n)

        lone = 0 if w == 0 else 5
        pairs_in_row = ((4, 5),) if w == 0 else ((0, 1),)
        for i in range(6):
            for j, j2 in pairs_in_row if s + 1 <= i <= s + 3 else ((0, 1), (2, 3), (4, 5)):
                add(layout.index((i, j)), layout.index((i, j2)), lambda n: row_pair(i, j, n))
        add(layout.index((s + 1, lone)), layout.index((s + 2, lone)), lambda n: column_pair(s + 1, lone, n))
        add(layout.index((s + 3, lone)), None, lambda n: column_pair(s + 3, lone, n))
        return acc

    def over_q(acc):
        parts = jnp.concatenate(high_low(jnp.concatenate(acc, 1)), 0)
        both = lax.dot_general(pick_row, parts, NT, preferred_element_type=F32)
        return both[0:4, 0:64] + both[0:4, 64:128]

    def far_leaf_sums(u, v):
        for s in range(2):
            for w in range(2):
                leaf = (2 * u + s) * 4 + 2 * v + w
                acc = far_sum(
                    s, w, lambda g: cl_v[leaf, g],
                    lambda i, j, n: leaf_row[2 * u + i, 2 * v + j, 4 + n : 5 + n, :],
                    lambda i, j, n: leaf_col[2 * u + i, 2 * v + j, 4 + n : 5 + n, :],
                )
                for n in range(4):
                    raw_far[leaf, n] = acc[n]

    def far_node_sums(box, s, w):
        return over_q(far_sum(
            s, w, lambda g: cn_v[box, g],
            lambda i, j, n: node_row[i, j, 4 + n : 5 + n, :],
            lambda i, j, n: node_col[i, j, 4 + n : 5 + n, :],
        ))

    def leaf_part(leaf, node_sum):
        far = over_q([raw_far[leaf, n] for n in range(4)])
        rows = stack_split(jnp.concatenate([far, node_sum], 1))
        down = jnp.concatenate([bas_v[leaf], g_v[leaf]], 0)
        near_y[leaf] = near_y[leaf] + split_dot(rows, down, NN)

    for leaf in range(16):
        if leaf not in (5, 6, 9, 10):
            near_y[leaf] = near_y[leaf] + near_sum(leaf, False)

    most = pl.ds(0, devices - 1)

    def all_but_one(buffer, sent, got):
        return pltpu.make_async_remote_copy(
            src_ref=buffer.at[most], dst_ref=buffer.at[most], send_sem=sent, recv_sem=got,
            device_id=others[0], device_id_type=MESH)

    all_but_one(table, ag_send, ag_recv).wait_recv()

    full = table[...]
    groups = full.reshape(n_x // 2, 2, n_y // 2, 2, 4, 128).sum(axis=(1, 3)).reshape(devices // 4, 4, 128)
    high = full.astype(BF16).astype(F32)
    tbl2[0:devices, 0:4, :] = high
    tbl2[0:devices, 4:8, :] = full - high
    high = groups.astype(BF16).astype(F32)
    tbl2[devices:, 0:4, :] = pltpu.roll(high, 64, 2)
    tbl2[devices:, 4:8, :] = pltpu.roll(groups - high, 64, 2)

    small[7].wait()
    for k in range(slots):
        stacked = tbl2[pairs_s[1, 0, k], :, 0:64].astype(BF16)
        prod[k * 8 : k * 8 + 4, 0:64] = fold(split_dot(stacked, cu_v[k], NT))

    for n in range(4):
        rows = prod[pl.ds(n, 40, stride=8), :][0:slots, 0:64]
        sums = []
        for pick in (pick_own, pick_parent):
            part = 0.0
            for piece in high_low(rows):
                part = part + lax.dot_general(pick, piece, NN, preferred_element_type=F32)
            sums.append(part)
        both = jnp.concatenate(sums, 1)
        rs_send[:, n : n + 1, :] = both.reshape(devices, 1, 128)

    for to_i, to_j in others:
        pltpu.make_async_remote_copy(
            src_ref=rs_send.at[to_i * n_y + to_j], dst_ref=rs_recv.at[me],
            send_sem=rs_sent, recv_sem=rs_got,
            device_id=(to_i, to_j), device_id_type=MESH).start()
    rs_recv[me] = rs_send[me]

    node_copy.wait()
    for leaf in range(16):
        cl_copy(leaf).wait()
    lax.fori_loop(0, 4, lambda k, c: (far_leaf_sums(lax.div(k, 2), lax.rem(k, 2)), c)[1], 0)
    for u in range(2):
        for v in range(2):
            node_sum = far_node_sums(2 * u + v, u, v)
            for s in range(2):
                for w in range(2):
                    leaf_part((2 * u + s) * 4 + 2 * v + w, node_sum)

    all_but_one(rs_recv, rs_sent, rs_got).wait_recv()
    sums = stack_split(jnp.sum(rs_recv[...], axis=0))

    down = lax.dot_general(sums, w_high[...], NN, preferred_element_type=F32)
    down = down + lax.dot_general(sums, w_low[...], NN, preferred_element_type=F32)
    for leaf in range(16):
        cols = slice(leaf * 128, leaf * 128 + 128)
        y_v[:, cols] = stack_split(fold(near_y[leaf] + down[:, cols])).astype(F32)

    total = jnp.zeros((128, 128), F32)
    for leaf in range(16):
        cols = slice(leaf * 128, leaf * 128 + 128)
        y = y_v[:, cols]
        spread = jnp.broadcast_to(y[None], (16, 8, 128)).reshape(128, 128)
        spread = jnp.where(row_group == order_high[:, cols], spread, 0.0).astype(BF16)
        total = total + lax.dot_general(spread, onehot_v[:, cols], NT, preferred_element_type=F32)
    for kh in range(16):
        out_ref[:, kh * 128 : kh * 128 + 128] = fold(total[kh * 8 : kh * 8 + 8])

    all_but_one(table, ag_send, ag_recv).wait_send()
    all_but_one(rs_send, rs_sent, rs_got).wait_send()
    for index, (dx, dy) in enumerate(DIRECTIONS):
        @pl.when(inside(dx, dy))
        def _(index=index):
            halo(index).wait_send()


def on_device(
    n_x, n_y,
    vectors, cluster_order, near_blocks, leaf_basis, couple_leaf, transfer_leaf,
    couple_node, transfer_node, transfer_device, couple_upper, pair_list,
):
    slots = couple_upper.shape[1]
    devices = n_x * n_y
    near = near_blocks.transpose(0, 1, 3, 2, 4).reshape(16, 9, 128, 128)
    basis = leaf_basis.transpose(0, 1, 3, 2).reshape(16, 64, 128)
    cl = couple_leaf.transpose(0, 1, 3, 2, 4).reshape(16, 27, 64, 64)
    cn = couple_node.transpose(0, 1, 3, 2, 4).reshape(4, 27, 64, 64)
    tl = transfer_leaf.reshape(16, 64, 64)
    tn = transfer_node.reshape(4, 64, 64)
    td = transfer_device.reshape(64, 64)
    cu = couple_upper.reshape(slots, 64, 64)
    dma = pltpu.SemaphoreType.DMA
    any_spec = pl.BlockSpec(memory_space=pl.ANY)
    return pl.pallas_call(
        functools.partial(kernel, n_x, n_y, slots),
        out_shape=jax.ShapeDtypeStruct((4, 2048), F32),
        in_specs=[any_spec] * 11 + [pl.BlockSpec(memory_space=pltpu.SMEM)],
        out_specs=pl.BlockSpec(memory_space=pltpu.VMEM),
        scratch_shapes=[
            pltpu.VMEM((4, 2048), F32),
            pltpu.VMEM((1, 2048), jnp.int32),
            pltpu.VMEM((16, 9, 128, 128), F32),
            pltpu.VMEM((16, 64, 128), F32),
            pltpu.VMEM((16, 27, 64, 64), F32),
            pltpu.VMEM((16, 64, 64), F32),
            pltpu.VMEM((4, 27, 64, 64), F32),
            pltpu.VMEM((4, 64, 64), F32),
            pltpu.VMEM((64, 64), F32),
            pltpu.VMEM((slots, 64, 64), F32),
            pltpu.VMEM((2, 1, slots), jnp.int32),
            pltpu.VMEM((128, 128), F32),
            pltpu.VMEM((128, 2048), BF16),
            pltpu.VMEM((8, 8, 8, 128), F32),
            pltpu.VMEM((6, 6, 8, 128), F32),
            pltpu.VMEM((8, 7, 8, 128), F32),
            pltpu.VMEM((7, 8, 8, 128), F32),
            pltpu.VMEM((6, 5, 8, 128), F32),
            pltpu.VMEM((5, 6, 8, 128), F32),
            pltpu.VMEM((4, 128), F32),
            pltpu.VMEM((devices, 4, 128), F32),
            pltpu.VMEM((devices + devices // 4, 8, 128), F32),
            pltpu.VMEM((320, 128), F32),
            pltpu.VMEM((devices, 4, 128), F32),
            pltpu.VMEM((devices, 4, 128), F32),
            pltpu.VMEM((16, 4, 64, 128), F32),
            pltpu.VMEM((16, 8, 128), F32),
            pltpu.VMEM((8, 2048), F32),
            pltpu.VMEM((16, 64, 128), F32),
            pltpu.VMEM((128, 2048), BF16),
            pltpu.VMEM((128, 2048), BF16),
            dma((8,)), dma((16,)), dma((16,)), dma(()),
            dma((8,)), dma((8,)), dma(()), dma(()), dma(()), dma(()),
        ],
        compiler_params=pltpu.CompilerParams(
            collective_id=0, has_side_effects=True, vmem_limit_bytes=56 * 1024 * 1024
        ),
    )(vectors, cluster_order, near, basis, cl, tl, cn, tn, td, cu, pair_list, pair_list)


def solution(mesh):
    in_specs = (
        P(None, ("gx", "gy")),
        P(("gx", "gy"), None),
        P("gx", "gy", None, None, None),
        P("gx", "gy", None, None),
        P("gx", "gy", None, None, None),
        P("gx", "gy", None, None),
        P("gx", "gy", None, None, None),
        P("gx", "gy", None, None),
        P("gx", "gy", None, None),
        P(("gx", "gy"), None, None, None),
        P(None, ("gx", "gy"), None),
    )
    out_specs = P(None, ("gx", "gy"))
    return jax.shard_map(
        functools.partial(on_device, mesh.shape["gx"], mesh.shape["gy"]),
        mesh=mesh, in_specs=in_specs, out_specs=out_specs, check_vma=False,
    )
```

```python
import functools

import jax
import jax.numpy as jnp
from jax import lax
from jax.experimental import pallas as pl
from jax.experimental.pallas import tpu as pltpu
from jax.sharding import PartitionSpec as P

F32 = jnp.float32
BF16 = jnp.bfloat16
MESH = pl.DeviceIdType.MESH
NT = (((1,), (1,)), ((), ()))
NN = (((1,), (0,)), ((), ()))
TN = (((0,), (0,)), ((), ()))
DIRECTIONS = [(dx, dy) for dx in (-1, 0, 1) for dy in (-1, 0, 1) if (dx, dy) != (0, 0)]


HOPS = (0, 1, 2, 1)
OFFSETS = sorted(
    [
        (x, y, z, c)
        for c in range(2)
        for x in range(4)
        for y in range(4)
        for z in range(4)
        if (x, y, z, c) != (0, 0, 0, 0)
    ],
    key=lambda o: -(HOPS[o[0]] + HOPS[o[1]] + HOPS[o[2]]),
)


def slots_of(s, w):
    return [
        (i, j)
        for i in range(6)
        for j in range(6)
        if not (s + 1 <= i <= s + 3 and w + 1 <= j <= w + 3)
    ]


def high_low(values):
    high = values.astype(BF16)
    return high, (values - high.astype(F32)).astype(BF16)


def stack_split(rows):
    high = rows.astype(BF16).astype(F32)
    return jnp.concatenate([high, rows - high], 0).astype(BF16)


def split_dot(stacked, matrix, dims):
    high, low = high_low(matrix)
    return lax.dot_general(stacked, high, dims, preferred_element_type=F32) + lax.dot_general(
        stacked, low, dims, preferred_element_type=F32
    )


def full_dot(left, matrix, dims):
    left_high, left_low = high_low(left)
    high, low = high_low(matrix)
    total = lax.dot_general(left_high, high, dims, preferred_element_type=F32)
    total = total + lax.dot_general(left_low, high, dims, preferred_element_type=F32)
    return total + lax.dot_general(left_high, low, dims, preferred_element_type=F32)


def fold(rows):
    return rows[0:4] + rows[4:8]


def kernel(
    n_x, n_y, slots,
    vec_h, ord_h, near_h, bas_h, cl_h, tl_h, cn_h, tn_h, td_h, cu_h, pairs_h, pairs_s,
    out_ref,
    vec_v, ord_v, near_v, bas_v, cl_v, tl_v, cn_v, tn_v, td_v, cu_v, pairs_v,
    vs_v, onehot_v, ext, xs_v, leaf_row, leaf_col, node_row, node_col, mine, table, tbl2, prod, rs_send, rs_recv,
    raw_far, near_y, y_v, g_v, w_high, w_low,
    small_sem, near_sem, cl_sem, cn_sem,
    halo_send, halo_recv, ag_send, ag_recv, rs_sent, rs_got,
):
    gi, gj = lax.axis_index("gx"), lax.axis_index("gy")
    devices = n_x * n_y
    me = gi * n_y + gj
    px, core, pz, py = lax.div(gi, 2), lax.rem(gi, 2), lax.div(gj, 4), lax.rem(gj, 4)
    others = []
    along_x = [[lax.rem(px + d, 4) * 2 + lax.rem(core + c, 2) for c in range(2)] for d in range(4)]
    along_zy = [[lax.rem(pz + z, 4) * 4 + lax.rem(py + y, 4) for y in range(4)] for z in range(4)]
    for dx, dy, dz, dc in OFFSETS:
        others.append((along_x[dx][dc], along_zy[dz][dy]))

    small = [
        pltpu.make_async_copy(src, dst, small_sem.at[k])
        for k, (src, dst) in enumerate([
            (vec_h, vec_v), (ord_h, ord_v), (bas_h, bas_v), (tl_h, tl_v), (tn_h, tn_v),
            (td_h, td_v), (pairs_h, pairs_v), (cu_h, cu_v),
        ])
    ]
    for copy in small:
        copy.start()

    ext[...] = jnp.zeros_like(ext)

    barrier = pltpu.get_barrier_semaphore()
    for other in others:
        pl.semaphore_signal(barrier, inc=1, device_id=other, device_id_type=MESH)

    node_copy = pltpu.make_async_copy(cn_h, cn_v, cn_sem)

    def cl_copy(leaf):
        return pltpu.make_async_copy(cl_h.at[leaf], cl_v.at[leaf], cl_sem.at[leaf])

    def near_copy(leaf):
        return pltpu.make_async_copy(near_h.at[leaf], near_v.at[leaf], near_sem.at[leaf])

    def start_cl(u):
        for v in range(2):
            for s in range(2):
                for w in range(2):
                    cl_copy((2 * u + s) * 4 + 2 * v + w).start()

    for leaf in range(16):
        near_copy(leaf).start()
    node_copy.start()
    start_cl(0)
    start_cl(1)

    def inside(dx, dy):
        ok = None
        for pos, step, count in ((gi, dx, n_x), (gj, dy, n_y)):
            if step == 0:
                continue
            here = pos + step < count if step > 0 else pos + step >= 0
            ok = here if ok is None else jnp.logical_and(ok, here)
        return ok

    small[0].wait()
    small[1].wait()
    vec = vec_v[...]
    vec_high = vec.astype(BF16).astype(F32)
    vec_low = vec - vec_high
    for kh in range(16):
        cols = slice(kh * 128, kh * 128 + 128)
        vs_v[kh * 8 : kh * 8 + 4, :] = vec_high[:, cols]
        vs_v[kh * 8 + 4 : kh * 8 + 8, :] = vec_low[:, cols]
    order = ord_v[...]
    order_low = jnp.bitwise_and(order, 127)
    order_high = lax.shift_right_logical(order, 7)
    sub = lax.broadcasted_iota(jnp.int32, (128, 128), 0)
    row_group = lax.shift_right_logical(sub, 3)
    vs = vs_v[...].astype(BF16)
    small[2].wait()
    for leaf in range(16):
        cols = slice(leaf * 128, leaf * 128 + 128)
        onehot = jnp.where(sub == order_low[:, cols], 1.0, 0.0).astype(BF16)
        onehot_v[:, cols] = onehot
        picked = lax.dot_general(vs, onehot, NN, preferred_element_type=F32)
        picked = jnp.where(row_group == order_high[:, cols], picked, 0.0)
        stacked = jnp.sum(picked.reshape(16, 8, 128), axis=0)
        up = fold(split_dot(stacked.astype(BF16), bas_v[leaf], NT))
        a, b = leaf // 4, leaf % 4
        ext[2 + a, 2 + b, 0:4, :] = fold(stacked)
        ext[2 + a, 2 + b, 4:8, 0:64] = up
        xs_v[1 + a, 1 + b] = stacked

    small[3].wait()
    small[4].wait()
    small[5].wait()
    up_device = jnp.zeros((8, 64), F32)
    for u in range(2):
        for v in range(2):
            node = jnp.zeros((8, 64), F32)
            for s in range(2):
                for w in range(2):
                    a, b = 2 * u + s, 2 * v + w
                    child = stack_split(ext[2 + a, 2 + b, 4:8, 0:64])
                    node = node + split_dot(child, tl_v[a * 4 + b], NN)
            node = fold(node)
            for p in range(2):
                for q in range(2):
                    ext[2 + 2 * p + u, 2 + 2 * q + v, 4:8, 64:128] = node
            up_device = up_device + split_dot(stack_split(node), tn_v[u * 2 + v], NN)
    up_device = fold(up_device)
    toward = fold(split_dot(stack_split(up_device), td_v[...], NN))
    mine[...] = jnp.concatenate([up_device, toward], 1)
    table[me] = mine[...]

    def near_sum(leaf, wanted):
        a, b = leaf // 4, leaf % 4
        rows, blocks = [], []
        for e in range(9):
            r, c = a + e // 3 - 1, b + e % 3 - 1
            if (0 <= r < 4 and 0 <= c < 4) == wanted:
                rows.append(xs_v[1 + r, 1 + c].astype(BF16))
                blocks.append(jnp.concatenate(high_low(near_v[leaf, e]), 0))
        if not rows:
            return jnp.zeros((8, 128), F32)
        both = lax.dot_general(
            jnp.concatenate(rows, 1), jnp.concatenate(blocks, 1), NT, preferred_element_type=F32
        )
        return both[:, 0:128] + both[:, 128:256]

    pl.semaphore_wait(barrier, devices - 1)

    for to in others:
        pltpu.make_async_remote_copy(
            src_ref=mine, dst_ref=table.at[me], send_sem=ag_send, recv_sem=ag_recv,
            device_id=to, device_id_type=MESH).start()

    cut = {-1: (2, 2, 6), 0: (2, 4, 2), 1: (4, 2, 0)}

    def halo(index):
        dx, dy = DIRECTIONS[index]
        (r0, rn, rd), (c0, cn, cd) = cut[dx], cut[dy]
        return pltpu.make_async_remote_copy(
            src_ref=ext.at[r0 : r0 + rn, c0 : c0 + cn], dst_ref=ext.at[rd : rd + rn, cd : cd + cn],
            send_sem=halo_send.at[index], recv_sem=halo_recv.at[index],
            device_id=(gi + dx, gj + dy), device_id_type=MESH)

    for index, (dx, dy) in enumerate(DIRECTIONS):
        @pl.when(inside(dx, dy))
        def _(index=index):
            halo(index).start()

    for leaf in range(16):
        near_copy(leaf).wait()
    for leaf in range(16):
        near_y[leaf] = near_sum(leaf, True)

    small[6].wait()
    target = pairs_v[0]
    row = lax.broadcasted_iota(jnp.int32, (devices, slots), 0)
    bits = n_y.bit_length() - 1
    half_i = lax.shift_right_logical(row, bits + 1)
    half_j = lax.shift_right_logical(jnp.bitwise_and(row, n_y - 1), 1)
    parent_box = devices + half_i * (n_y // 2) + half_j
    pick_own = jnp.where(row == target, 1.0, 0.0).astype(BF16)
    pick_parent = jnp.where(parent_box == target, 1.0, 0.0).astype(BF16)

    for u in range(2):
        for v in range(2):
            family = [(2 * u + s) * 4 + 2 * v + w for s in range(2) for w in range(2)]
            steps = [full_dot(tl_v[leaf], bas_v[leaf], TN) for leaf in family]
            for leaf, step in zip(family, steps):
                g_v[leaf] = step
            down = full_dot(tn_v[u * 2 + v], jnp.concatenate(steps, 1), TN)
            both = jnp.concatenate([down, full_dot(td_v[...], down, TN)], 0)
            high, low = high_low(both)
            for k, leaf in enumerate(family):
                cols = slice(leaf * 128, leaf * 128 + 128)
                w_high[:, cols] = high[:, k * 128 : k * 128 + 128]
                w_low[:, cols] = low[:, k * 128 : k * 128 + 128]

    most = pl.ds(0, devices - 1)

    def all_but_one(buffer, sent, got):
        return pltpu.make_async_remote_copy(
            src_ref=buffer.at[most], dst_ref=buffer.at[most], send_sem=sent, recv_sem=got,
            device_id=others[0], device_id_type=MESH)

    all_but_one(table, ag_send, ag_recv).wait_recv()

    full = table[...]
    groups = full.reshape(n_x // 2, 2, n_y // 2, 2, 4, 128).sum(axis=(1, 3)).reshape(devices // 4, 4, 128)
    high = full.astype(BF16).astype(F32)
    tbl2[0:devices, 0:4, :] = high
    tbl2[0:devices, 4:8, :] = full - high
    high = groups.astype(BF16).astype(F32)
    tbl2[devices:, 0:4, :] = pltpu.roll(high, 64, 2)
    tbl2[devices:, 4:8, :] = pltpu.roll(groups - high, 64, 2)

    small[7].wait()
    for k in range(slots):
        stacked = tbl2[pairs_s[1, 0, k], :, 0:64].astype(BF16)
        prod[k * 8 : k * 8 + 4, 0:64] = fold(split_dot(stacked, cu_v[k], NT))

    for n in range(4):
        rows = prod[pl.ds(n, 40, stride=8), :][0:slots, 0:64]
        sums = []
        for pick in (pick_own, pick_parent):
            part = 0.0
            for piece in high_low(rows):
                part = part + lax.dot_general(pick, piece, NN, preferred_element_type=F32)
            sums.append(part)
        both = jnp.concatenate(sums, 1)
        rs_send[:, n : n + 1, :] = both.reshape(devices, 1, 128)

    for to_i, to_j in others:
        pltpu.make_async_remote_copy(
            src_ref=rs_send.at[to_i * n_y + to_j], dst_ref=rs_recv.at[me],
            send_sem=rs_sent, recv_sem=rs_got,
            device_id=(to_i, to_j), device_id_type=MESH).start()
    rs_recv[me] = rs_send[me]

    for index, (dx, dy) in enumerate(DIRECTIONS):
        @pl.when(inside(dx, dy))
        def _(dx=dx, dy=dy):
            halo(DIRECTIONS.index((-dx, -dy))).wait_recv()

    for r in range(6):
        for c in range(6):
            if not (1 <= r <= 4 and 1 <= c <= 4):
                x = ext[r + 1, c + 1, 0:4, :]
                high = x.astype(BF16).astype(F32)
                xs_v[r, c, 0:4, :] = high
                xs_v[r, c, 4:8, :] = x - high

    lane = lax.broadcasted_iota(jnp.int32, (8, 128), 1)

    def side_by_side(left, right):
        return jnp.where(lane < 64, left, right)

    node_at = (0, 1, 2, 3, 6, 7)
    for r in range(8):
        for c in range(8):
            swapped = pltpu.roll(ext[r, c], 64, 1)
            if c > 0:
                leaf_row[r, c - 1] = side_by_side(ext[r, c - 1], swapped)
            if r > 0:
                leaf_col[r - 1, c] = side_by_side(ext[r - 1, c], swapped)
    for r in range(6):
        for c in range(6):
            here = ext[node_at[r], node_at[c]]
            swapped = pltpu.roll(here, 64, 1)
            if c < 5:
                node_row[r, c] = side_by_side(swapped, ext[node_at[r], node_at[c + 1]])
            if r < 5:
                node_col[r, c] = side_by_side(swapped, ext[node_at[r + 1], node_at[c]])

    row8 = lax.broadcasted_iota(jnp.int32, (8, 512), 0)
    group8 = lax.shift_right_logical(lax.broadcasted_iota(jnp.int32, (8, 512), 1), 7)
    pick_row = jnp.where(row8 == group8, 1.0, 0.0).astype(BF16)

    def far_sum(s, w, blocks, row_pair, column_pair):
        layout = slots_of(s, w)
        acc = [jnp.zeros((64, 128), F32) for _ in range(4)]

        def add(left, right, source):
            pair = jnp.concatenate([blocks(left), jnp.zeros((64, 64), F32) if right is None else blocks(right)], 1)
            for n in range(4):
                acc[n] = acc[n] + pair * source(n)

        lone = 0 if w == 0 else 5
        pairs_in_row = ((4, 5),) if w == 0 else ((0, 1),)
        for i in range(6):
            for j, j2 in pairs_in_row if s + 1 <= i <= s + 3 else ((0, 1), (2, 3), (4, 5)):
                add(layout.index((i, j)), layout.index((i, j2)), lambda n: row_pair(i, j, n))
        add(layout.index((s + 1, lone)), layout.index((s + 2, lone)), lambda n: column_pair(s + 1, lone, n))
        add(layout.index((s + 3, lone)), None, lambda n: column_pair(s + 3, lone, n))
        return acc

    def over_q(acc):
        parts = jnp.concatenate(high_low(jnp.concatenate(acc, 1)), 0)
        both = lax.dot_general(pick_row, parts, NT, preferred_element_type=F32)
        return both[0:4, 0:64] + both[0:4, 64:128]

    def far_leaf_sums(u, v):
        for s in range(2):
            for w in range(2):
                leaf = (2 * u + s) * 4 + 2 * v + w
                acc = far_sum(
                    s, w, lambda g: cl_v[leaf, g],
                    lambda i, j, n: leaf_row[2 * u + i, 2 * v + j, 4 + n : 5 + n, :],
                    lambda i, j, n: leaf_col[2 * u + i, 2 * v + j, 4 + n : 5 + n, :],
                )
                for n in range(4):
                    raw_far[leaf, n] = acc[n]

    def far_node_sums(box, s, w):
        return over_q(far_sum(
            s, w, lambda g: cn_v[box, g],
            lambda i, j, n: node_row[i, j, 4 + n : 5 + n, :],
            lambda i, j, n: node_col[i, j, 4 + n : 5 + n, :],
        ))

    def leaf_part(leaf, node_sum):
        far = over_q([raw_far[leaf, n] for n in range(4)])
        rows = stack_split(jnp.concatenate([far, node_sum], 1))
        down = jnp.concatenate([bas_v[leaf], g_v[leaf]], 0)
        near_y[leaf] = near_y[leaf] + split_dot(rows, down, NN)

    for leaf in range(16):
        if leaf not in (5, 6, 9, 10):
            near_y[leaf] = near_y[leaf] + near_sum(leaf, False)

    node_copy.wait()
    for leaf in range(16):
        cl_copy(leaf).wait()
    lax.fori_loop(0, 4, lambda k, c: (far_leaf_sums(lax.div(k, 2), lax.rem(k, 2)), c)[1], 0)
    for u in range(2):
        for v in range(2):
            node_sum = far_node_sums(2 * u + v, u, v)
            for s in range(2):
                for w in range(2):
                    leaf_part((2 * u + s) * 4 + 2 * v + w, node_sum)

    all_but_one(rs_recv, rs_sent, rs_got).wait_recv()
    sums = stack_split(jnp.sum(rs_recv[...], axis=0))

    down = lax.dot_general(sums, w_high[...], NN, preferred_element_type=F32)
    down = down + lax.dot_general(sums, w_low[...], NN, preferred_element_type=F32)
    for leaf in range(16):
        cols = slice(leaf * 128, leaf * 128 + 128)
        y_v[:, cols] = stack_split(fold(near_y[leaf] + down[:, cols])).astype(F32)

    total = jnp.zeros((128, 128), F32)
    for leaf in range(16):
        cols = slice(leaf * 128, leaf * 128 + 128)
        y = y_v[:, cols]
        spread = jnp.broadcast_to(y[None], (16, 8, 128)).reshape(128, 128)
        spread = jnp.where(row_group == order_high[:, cols], spread, 0.0).astype(BF16)
        total = total + lax.dot_general(spread, onehot_v[:, cols], NT, preferred_element_type=F32)
    for kh in range(16):
        out_ref[:, kh * 128 : kh * 128 + 128] = fold(total[kh * 8 : kh * 8 + 8])

    all_but_one(table, ag_send, ag_recv).wait_send()
    all_but_one(rs_send, rs_sent, rs_got).wait_send()
    for index, (dx, dy) in enumerate(DIRECTIONS):
        @pl.when(inside(dx, dy))
        def _(index=index):
            halo(index).wait_send()


def on_device(
    n_x, n_y,
    vectors, cluster_order, near_blocks, leaf_basis, couple_leaf, transfer_leaf,
    couple_node, transfer_node, transfer_device, couple_upper, pair_list,
):
    slots = couple_upper.shape[1]
    devices = n_x * n_y
    near = near_blocks.transpose(0, 1, 3, 2, 4).reshape(16, 9, 128, 128)
    basis = leaf_basis.transpose(0, 1, 3, 2).reshape(16, 64, 128)
    cl = couple_leaf.transpose(0, 1, 3, 2, 4).reshape(16, 27, 64, 64)
    cn = couple_node.transpose(0, 1, 3, 2, 4).reshape(4, 27, 64, 64)
    tl = transfer_leaf.reshape(16, 64, 64)
    tn = transfer_node.reshape(4, 64, 64)
    td = transfer_device.reshape(64, 64)
    cu = couple_upper.reshape(slots, 64, 64)
    dma = pltpu.SemaphoreType.DMA
    any_spec = pl.BlockSpec(memory_space=pl.ANY)
    return pl.pallas_call(
        functools.partial(kernel, n_x, n_y, slots),
        out_shape=jax.ShapeDtypeStruct((4, 2048), F32),
        in_specs=[any_spec] * 11 + [pl.BlockSpec(memory_space=pltpu.SMEM)],
        out_specs=pl.BlockSpec(memory_space=pltpu.VMEM),
        scratch_shapes=[
            pltpu.VMEM((4, 2048), F32),
            pltpu.VMEM((1, 2048), jnp.int32),
            pltpu.VMEM((16, 9, 128, 128), F32),
            pltpu.VMEM((16, 64, 128), F32),
            pltpu.VMEM((16, 27, 64, 64), F32),
            pltpu.VMEM((16, 64, 64), F32),
            pltpu.VMEM((4, 27, 64, 64), F32),
            pltpu.VMEM((4, 64, 64), F32),
            pltpu.VMEM((64, 64), F32),
            pltpu.VMEM((slots, 64, 64), F32),
            pltpu.VMEM((2, 1, slots), jnp.int32),
            pltpu.VMEM((128, 128), F32),
            pltpu.VMEM((128, 2048), BF16),
            pltpu.VMEM((8, 8, 8, 128), F32),
            pltpu.VMEM((6, 6, 8, 128), F32),
            pltpu.VMEM((8, 7, 8, 128), F32),
            pltpu.VMEM((7, 8, 8, 128), F32),
            pltpu.VMEM((6, 5, 8, 128), F32),
            pltpu.VMEM((5, 6, 8, 128), F32),
            pltpu.VMEM((4, 128), F32),
            pltpu.VMEM((devices, 4, 128), F32),
            pltpu.VMEM((devices + devices // 4, 8, 128), F32),
            pltpu.VMEM((320, 128), F32),
            pltpu.VMEM((devices, 4, 128), F32),
            pltpu.VMEM((devices, 4, 128), F32),
            pltpu.VMEM((16, 4, 64, 128), F32),
            pltpu.VMEM((16, 8, 128), F32),
            pltpu.VMEM((8, 2048), F32),
            pltpu.VMEM((16, 64, 128), F32),
            pltpu.VMEM((128, 2048), BF16),
            pltpu.VMEM((128, 2048), BF16),
            dma((8,)), dma((16,)), dma((16,)), dma(()),
            dma((8,)), dma((8,)), dma(()), dma(()), dma(()), dma(()),
        ],
        compiler_params=pltpu.CompilerParams(
            collective_id=0, has_side_effects=True, vmem_limit_bytes=56 * 1024 * 1024
        ),
    )(vectors, cluster_order, near, basis, cl, tl, cn, tn, td, cu, pair_list, pair_list)


def solution(mesh):
    in_specs = (
        P(None, ("gx", "gy")),
        P(("gx", "gy"), None),
        P("gx", "gy", None, None, None),
        P("gx", "gy", None, None),
        P("gx", "gy", None, None, None),
        P("gx", "gy", None, None),
        P("gx", "gy", None, None, None),
        P("gx", "gy", None, None),
        P("gx", "gy", None, None),
        P(("gx", "gy"), None, None, None),
        P(None, ("gx", "gy"), None),
    )
    out_specs = P(None, ("gx", "gy"))
    return jax.shard_map(
        functools.partial(on_device, mesh.shape["gx"], mesh.shape["gy"]),
        mesh=mesh, in_specs=in_specs, out_specs=out_specs, check_vma=False,
    )
```
